512 devices in a mesh: expert: 64 (over x, y, core), store: 8 (over z).
Axes of the slice: x: 4, y: 8, z: 8, core: 2. Of those that a mesh axis runs over, the one named last changes fastest.
Arguments:
- tokens: bfloat16 [65536, 2048], P(('expert', 'store')), may hold values from -6 to 6
- chosen_expert_index: int32 [65536, 8], P(('expert', 'store')), may hold values from 0 to 63, all different within a row; in each aligned block of 128 rows (0 to 127, 128 to 255, ...) at most 18 rows name the same one
- router_weight_logits: float32 [65536, 8], P(('expert', 'store')), may hold values from 0.1 to 1
- token_tenant_index: int32 [65536], P(('expert', 'store')), may hold values from 0 to 7
- adapted: int32 [8, 64], P(None, 'expert'), may hold values 0 or 1
- gate_up_weight: bfloat16 [64, 2048, 768], P('expert', 'store'), may hold values from -0.125 to 0.125
- down_weight: bfloat16 [64, 384, 2048], P('expert', None, 'store'), may hold values from -0.3125 to 0.3125
- adapter_input_factors: bfloat16 [8, 64, 32, 2048], P('store', 'expert'), may hold values from -0.125 to 0.125
- adapter_output_factors: bfloat16 [8, 64, 32, 384], P('store', 'expert'), may hold values from -0.8984375 to 0.8984375
Outputs:
- mixed: bfloat16 [65536, 2048], P(('expert', 'store'))
The draws below stay inside these ranges and needn't reach their ends.
Inputs may be any that keep to these rules, and one draw needn't show every extreme that they name: `chosen_expert_index`: each row names 8 different experts; within the rows of one device no expert is named by more than 18 rows.
All inputs are finite; a program needn't handle non-finite values. No bound on the sum of `adapted` on one device may be relied on, other than what follows from the above.
Results may differ from the reference program's by a relative error of at most 0.006.
Values may be sent and summed in bfloat16 or wider, within the bound.
A program may use at most 128 MiB of HBM per device.

```python
import math
import jax
import jax.numpy as jnp
import numpy as np
from jax import lax

MODEL_DIMENSION = 2048
EXPERT_HIDDEN = 384
ADAPTER_RANK = 16
TOPK = 8
TOK_DEV = 128
EXPERT_TOTAL = 64
CAP = 18
TENANT_TOTAL = 8
TOKENS = 65536


def touch_ends(drawn, key, smallest, top_value):
    dims = drawn.shape
    spot = [jax.random.randint(jax.random.fold_in(key, axis), (), 0, dims[axis]) for axis in range(len(dims))]
    drawn = drawn.at[tuple(spot)].set(smallest)
    longest = dims.index(max(dims))
    spot[longest] = (spot[longest] + 1) % dims[longest]
    return drawn.at[tuple(spot)].set(top_value)


def block_levels(key, extent, cuts, low, high):
    def one(dim, shards_of):
        heights = jax.random.uniform(jax.random.fold_in(jax.random.fold_in(key, 6), dim), (shards_of,), jnp.float32, low / len(cuts), high / len(cuts))
        return jnp.repeat(jnp.exp(heights), extent[dim] // shards_of).reshape((-1,) + (1,) * (len(extent) - dim - 1))

    loudness = one(*cuts[0])
    for cut in cuts[1:]:
        loudness = loudness * one(*cut)
    return loudness


def deal_out(key, own, number, rows, amount, top, bound, slope):
    order = jax.random.permutation(key, amount)
    crowded, usual = portions_of(amount, rows * top, bound, slope, True), portions_of(amount, rows * top, bound, slope, False)
    places = jnp.arange(amount)

    def named(tallies, turn):
        used = int((tallies > 0).sum())
        fixed = max(1, used // 4)
        moved = fixed + (places - fixed + turn * (used - fixed)) % max(1, amount - fixed)
        return jnp.zeros((amount,), jnp.int32).at[order[jnp.where(places < fixed, places, moved)]].set(jnp.asarray(tallies, jnp.int32))

    tallies = jnp.where(number % 4 == 0, named(crowded, number // 4), named(usual, number - number // 4 - 1))
    mixed = jax.random.permutation(jax.random.fold_in(own, 3), amount)
    giver, taker = mixed[0:amount // 2 * 2:2], mixed[1:amount // 2 * 2:2]
    margin = jnp.minimum(tallies[giver] - 1, bound - tallies[taker]) // 2
    margin = jnp.where((giver == order[0]) | (taker == order[0]) | (tallies[taker] == 0), 0, jnp.maximum(margin, 0))
    moved = jax.random.randint(jax.random.fold_in(own, 4), (amount // 2,), 0, 1 << 20) % (margin + 1)
    tallies = tallies.at[giver].add(-moved).at[taker].add(moved)
    items = jnp.searchsorted(jnp.cumsum(tallies), jnp.arange(rows * top), side="right").astype(jnp.int32)
    table = items.reshape(top, rows).T
    table = table[jax.random.permutation(jax.random.fold_in(own, 1), rows)]
    turn = jax.random.randint(jax.random.fold_in(own, 2), (rows, 1), 0, top)
    return jnp.take_along_axis(table, (jnp.arange(top)[None, :] + turn) % top, axis=1)


def portions_of(count, total, most, lean, full):
    loads = [(1 << 20) // math.isqrt(rank ** lean) + 1 for rank in range(1, count + 1)]
    largest = most if full else min(most, max(-(-total // count), total * loads[0] // sum(loads)))
    least = 1 if total - largest >= count - 1 else 0
    counts, surplus = [largest] + [least] * (count - 1), total - largest - least * (count - 1)
    while surplus > 0:
        movable = [i for i in range(1, count) if counts[i] < largest] or [i for i in range(1, count) if counts[i] < most]
        whole, budget = sum([loads[i] for i in movable]), surplus
        for i in movable:
            addition = min(most - counts[i], max(1, budget * loads[i] // whole), surplus)
            counts[i] = counts[i] + addition
            surplus = surplus - addition
    return np.array(counts)


def bell_draw(key, dims, spread, most, cuts=(), held_as=jnp.bfloat16):
    values = jax.random.normal(key, dims, jnp.float32) * spread
    if len(cuts) > 0:
        values = block_levels(key, dims, cuts, -0.22, 0.18) * values
    return jnp.clip(values, min=-most, max=most).astype(held_as)


def setup_inputs(seed: int = 0) -> dict:
    streams_of = jax.random.split(jax.random.key(seed), 10)
    tokens = bell_draw(streams_of[0], (TOKENS, MODEL_DIMENSION), 1.0, 6.0, ((0, 512),))
    chosen_expert_index_keys = jax.random.split(jax.random.fold_in(streams_of[1], 1), TOKENS // TOK_DEV)
    chosen_expert_index_turns = jax.random.permutation(jax.random.fold_in(streams_of[1], 3), TOKENS // TOK_DEV)
    chosen_expert_index = jax.vmap(lambda own, number: deal_out(jax.random.fold_in(streams_of[1], 2), own, number, TOK_DEV, EXPERT_TOTAL, TOPK, CAP, 2))(chosen_expert_index_keys, chosen_expert_index_turns).reshape((TOKENS, TOPK))
    router_weight_logits = jnp.clip(jnp.exp(math.log(1.0) - 2.3025851 * jax.random.uniform(streams_of[2], (TOKENS, TOPK), jnp.float32) ** block_levels(streams_of[2], (TOKENS, TOPK), ((0, 512),), -0.2, 0.2)), 0.1, 1.0)
    token_tenant_index = touch_ends(jax.random.randint(streams_of[3], (TOKENS,), 0, TENANT_TOTAL), jax.random.fold_in(streams_of[3], 1), 0, TENANT_TOTAL - 1).astype(jnp.int32)
    adapted = touch_ends((jax.random.randint(streams_of[4], (TENANT_TOTAL, EXPERT_TOTAL), 0, 4) < 3).astype(jnp.int32), jax.random.fold_in(streams_of[4], 1), 0, 1)
    gate_up_weight = bell_draw(streams_of[5], (EXPERT_TOTAL, MODEL_DIMENSION, 2 * EXPERT_HIDDEN), MODEL_DIMENSION ** -0.5, 0.125, ((0, 64), (1, 8)))
    down_weight = bell_draw(streams_of[6], (EXPERT_TOTAL, EXPERT_HIDDEN, MODEL_DIMENSION), EXPERT_HIDDEN ** -0.5, 0.3125, ((0, 64), (2, 8)))
    adapter_input_factors = bell_draw(streams_of[7], (TENANT_TOTAL, EXPERT_TOTAL, 2 * ADAPTER_RANK, MODEL_DIMENSION), MODEL_DIMENSION ** -0.5, 0.125, ((0, 8), (1, 64)))
    adapter_output_factors = bell_draw(streams_of[8], (TENANT_TOTAL, EXPERT_TOTAL, 2 * ADAPTER_RANK, EXPERT_HIDDEN), 0.15, 0.8984375, ((0, 8), (1, 64)))
    return dict(tokens=tokens, chosen_expert_index=chosen_expert_index, router_weight_logits=router_weight_logits, token_tenant_index=token_tenant_index, adapted=adapted, gate_up_weight=gate_up_weight, down_weight=down_weight, adapter_input_factors=adapter_input_factors, adapter_output_factors=adapter_output_factors)


def widen_factors(factor_up):
    rank_half = factor_up.shape[1] // 2
    hidden = factor_up.shape[2]
    zeros_part = jnp.zeros((factor_up.shape[0], rank_half, hidden), factor_up.dtype)
    upper = jnp.concatenate([factor_up[:, :rank_half], zeros_part], axis=2)
    lower = jnp.concatenate([zeros_part, factor_up[:, rank_half:]], axis=2)
    return jnp.concatenate([upper, lower], axis=1).reshape(-1, 2 * hidden)


def adapter_term(flat_rows, tenant_codes, factor_in, factor_up, adapted_col):
    tenants = factor_in.shape[0]
    rank_full = factor_in.shape[1]
    model_width = factor_in.shape[2]
    low_rank = lax.dot_general(flat_rows, factor_in.reshape(-1, model_width), (((1,), (1,)), ((), ())), preferred_element_type=jnp.float32)
    chooser = ((tenant_codes[:, None] == jnp.arange(tenants, dtype=jnp.int32)[None, :]) * adapted_col[None, :]).astype(jnp.float32)
    low_rank = (low_rank.reshape(-1, tenants, rank_full) * chooser[:, :, None]).reshape(flat_rows.shape[0], -1).astype(jnp.bfloat16)
    return jnp.dot(low_rank, widen_factors(factor_up), preferred_element_type=jnp.float32)


def reference(tokens, chosen_expert_index, router_weight_logits, token_tenant_index, adapted, gate_up_weight, down_weight, adapter_input_factors, adapter_output_factors):
    tok_total, model_width = tokens.shape
    experts = gate_up_weight.shape[0]
    hidden = down_weight.shape[1]
    blocks = tok_total // TOK_DEV
    per_block = TOK_DEV * TOPK
    block_ids = chosen_expert_index.reshape(blocks, per_block)
    onehot = (block_ids[:, :, None] == jnp.arange(experts, dtype=jnp.int32)[None, None, :]).astype(jnp.int32)
    position = jnp.sum((jnp.cumsum(onehot, axis=1) - 1) * onehot, axis=2)
    slot_index = block_ids * (blocks * CAP) + jnp.arange(blocks, dtype=jnp.int32)[:, None] * CAP + position
    route_rows = tok_total * TOPK
    position_row = jnp.full((experts * blocks * CAP,), route_rows, jnp.int32)
    position_row = position_row.at[slot_index.reshape(-1)].set(jnp.arange(route_rows, dtype=jnp.int32)).reshape(experts, blocks * CAP)
    shares = router_weight_logits / jnp.sum(router_weight_logits, axis=1, keepdims=True)
    share_flat = jnp.concatenate([shares.reshape(-1), jnp.zeros((1,), jnp.float32)])
    padded = jnp.concatenate([tokens, jnp.zeros((1, model_width), tokens.dtype)])
    tenant_pad = jnp.concatenate([token_tenant_index, jnp.full((1,), -1, jnp.int32)])

    def expert_step(accum, inputs):
        row_index, weight_in, weight_out, factor_in, factor_up, adapted_col = inputs
        token_index = row_index // TOPK
        flat_rows = padded[token_index]
        pre_act = jnp.dot(flat_rows, weight_in, preferred_element_type=jnp.float32)
        pre_act = pre_act + adapter_term(flat_rows, tenant_pad[token_index], factor_in, factor_up, adapted_col)
        activation = (jax.nn.silu(pre_act[:, :hidden]) * pre_act[:, hidden:]).astype(jnp.bfloat16)
        expert_out = jnp.dot(activation, weight_out, preferred_element_type=jnp.float32).astype(jnp.bfloat16)
        contribution = expert_out.astype(jnp.float32) * share_flat[row_index][:, None]
        return accum.at[token_index].add(contribution), None

    accum = jnp.zeros((tok_total + 1, model_width), jnp.float32)
    stacked_rows = (position_row, gate_up_weight, down_weight, jnp.swapaxes(adapter_input_factors, 0, 1), jnp.swapaxes(adapter_output_factors, 0, 1), jnp.swapaxes(adapted, 0, 1))
    accum, unused = lax.scan(expert_step, accum, stacked_rows)
    return accum[:tok_total].astype(jnp.bfloat16)
```

```python
import functools

import jax
import jax.numpy as jnp
from jax import lax
from jax.experimental import pallas as pl
from jax.experimental.pallas import tpu as pltpu
from jax.sharding import PartitionSpec as P

MESH = pl.DeviceIdType.MESH
NX, NY, NC = 4, 8, 2
PEERS = NX * NC
SLOTS = 18
TILE = 16
CHUNKS = 8
GROUP = 4
F32, BF16 = jnp.float32, jnp.bfloat16


def dot(a, b, dims=((1,), (0,))):
    return lax.dot_general(a, b, (dims, ((), ())), preferred_element_type=F32)


def chunk_column(step, z):
    far = (step + 1) // 2
    return jnp.where(step % 2 == 1, z - far + 8, z + far) % 8


def layer_kernel(
    tok_ref, idx_ref, logit_ref, ten_ref, adp_ref, win_ref, wout_ref, fin_ref, fup_ref, out_ref,
    tokbuf, meta, sel, mix, xsend, xrecv, code_s, code_r, winb, woutb, finb, fupb, wide, pre, act,
    xret, part, rs_s, rs_r,
    y_ss, y_rs, m_ss, m_rs, x_ss, x_rs, c_ss, c_rs, w_ss, w_rs, b_ss, b_rs, r_ss, r_rs,
):
    toks = tok_ref.shape[0]
    topk = idx_ref.shape[0]
    width = tok_ref.shape[1] // CHUNKS
    hidden = wout_ref.shape[0]
    rank = fin_ref.shape[0]
    block = NY * SLOTS
    half = toks // 2
    e = lax.axis_index("expert")
    z = lax.axis_index("store")
    x, y, c = e // (NY * NC), (e // NC) % NY, e % NC

    def at(dx, dy, dc):
        return (((x + dx) % NX * NY + (y + dy) % NY) * NC + (c + dc) % NC, z)

    def away(p):
        return at(p // NC, 0, p % NC)

    def back(p):
        return at(NX - p // NC, 0, p % NC)

    ring = (at(0, 1, 0), at(0, NY - 1, 0))
    zring = ((e, (z + 1) % 8), (e, (z + 7) % 8))

    def remote(src, dst, ss, rs, dev):
        return pltpu.make_async_remote_copy(
            src_ref=src, dst_ref=dst, send_sem=ss, recv_sem=rs, device_id=dev, device_id_type=MESH
        )

    barrier = pltpu.get_barrier_semaphore()
    partners = [*ring, *zring] + [away(p) for p in range(1, PEERS)]
    for dev in partners:
        pl.semaphore_signal(barrier, inc=1, device_id=dev, device_id_type=MESH)

    winb[z] = win_ref[...]
    woutb[z] = wout_ref[...]
    fupb[z] = fup_ref[...]
    for k in range(CHUNKS):
        finb[z, k] = fin_ref[:, k * width : (k + 1) * width]

    def take(k, _):
        col = pl.multiple_of(chunk_column(k, z) * width, width)
        tokbuf[k, 0] = tok_ref[:, pl.ds(col, width)]
        return 0

    lax.fori_loop(0, CHUNKS, take, 0)

    ids = idx_ref[...]
    experts = NX * NY * NC
    named = lax.broadcasted_iota(jnp.int32, (experts, toks), 0)
    chosen = jnp.zeros((experts, toks), F32)
    for k in range(topk):
        chosen = chosen + jnp.where(ids[k : k + 1, :] == named, 1.0, 0.0)
    before = jnp.where(
        lax.broadcasted_iota(jnp.int32, (toks, toks), 0)
        < lax.broadcasted_iota(jnp.int32, (toks, toks), 1),
        1.0,
        0.0,
    ).astype(BF16)
    rank_of = dot(chosen.astype(BF16), before)
    peer = (((ids // (NY * NC)) - x + NX) % NX) * NC + (ids % NC + c) % NC
    place = ((ids // NC) % NY * 256 + peer * 32).astype(F32)
    for k in range(topk):
        slot = jnp.sum(jnp.where(ids[k : k + 1, :] == named, rank_of, 0.0), axis=0, keepdims=True)
        meta[0, k : k + 1, :] = place[k : k + 1, :] + slot
    logits = logit_ref[...]
    meta[0, topk : 2 * topk, :] = logits / jnp.sum(logits, axis=0, keepdims=True)
    meta[0, 2 * topk : 3 * topk, :] = jnp.broadcast_to(ten_ref[...], (topk, toks)).astype(F32)

    pl.semaphore_wait(barrier, len(partners))

    def zcopies(kind, h):
        out = []
        for d in range(2):
            src_z = (z - (h - 1) + 8) % 8 if d == 0 else (z + (h - 1)) % 8
            ss, rs = w_ss.at[kind, h - 1, d], w_rs.at[kind, h - 1, d]
            ref = (finb, fupb, winb, woutb)[kind].at[src_z]
            if h == 4:
                n = ref.shape[0] // 2
                ref = ref.at[pl.ds(d * n, n)]
            out.append((ref, ss, rs, d))
        return out

    def zsend(kind, h):
        for ref, ss, rs, d in zcopies(kind, h):
            remote(ref, ref, ss, rs, zring[d]).start()

    def zarrive(kind, h):
        for ref, ss, rs, d in zcopies(kind, h):
            remote(ref, ref, ss, rs, zring[d]).wait_recv()

    def zsent(kind, h):
        for ref, ss, rs, d in zcopies(kind, h):
            remote(ref, ref, ss, rs, zring[d]).wait_send()

    def place_of(h, d):
        return 0 if h == 0 else (7 if h == 4 else 2 * h - 1 + d)

    def ycopy(k, h, d):
        src, dst = tokbuf.at[k, place_of(h - 1, d)], tokbuf.at[k, place_of(h, d)]
        if h == 4:
            src, dst = src.at[pl.ds(d * half, half)], dst.at[pl.ds(d * half, half)]
        return remote(src, dst, y_ss.at[k, h - 1, d], y_rs.at[k, h - 1, d], ring[d])

    def mcopy(h, d):
        src, dst = meta.at[place_of(h - 1, d)], meta.at[place_of(h, d)]
        return remote(src, dst, m_ss.at[h - 1, d], m_rs.at[h - 1, d], ring[d])

    def hops_of_meta(h):
        return (0,) if h == 4 else (0, 1)

    row_no = lax.broadcasted_iota(jnp.int32, (256, toks), 0)

    def build(q):
        want = (row_no + (y * 256 - 2 * q)).astype(F32)
        hot = jnp.zeros((256, toks), F32)
        share = jnp.zeros((256, toks), F32)
        for k in range(topk):
            same = meta[q, k : k + 1, :] == want
            hot = jnp.where(same, 1.0, hot)
            share = jnp.where(same, meta[q, topk + k : topk + k + 1, :], share)
        hot = hot.astype(BF16).reshape(PEERS, 2, TILE, toks)
        sel[q, :, toks : 2 * toks] = hot[:, 0].reshape(PEERS * TILE, toks)
        sel[q + 1, :, 0:toks] = hot[:, 1].reshape(PEERS * TILE, toks)
        share = share.T
        high = share.astype(BF16)
        mix[q, 0:toks] = high
        mix[q, toks : 2 * toks] = (share - high.astype(F32)).astype(BF16)

    def tenants():
        lane_of = lax.broadcasted_iota(jnp.int32, (TILE, toks), 0)
        codes = jnp.zeros((TILE, PEERS * TILE), F32)
        for i in range(NY + 1):
            mine = lane_of == i
            if i > 0:
                v = jnp.where(mine, meta[i - 1, 2 * topk : 2 * topk + 1, :], 0.0).astype(BF16)
                codes = codes + dot(v, sel[i, :, 0:toks], ((1,), (1,)))
            if i < NY:
                v = jnp.where(mine, meta[i, 2 * topk : 2 * topk + 1, :], 0.0).astype(BF16)
                codes = codes + dot(v, sel[i, :, toks : 2 * toks], ((1,), (1,)))
        code_s[...] = codes.astype(BF16)
        code_r[0] = codes.astype(BF16)

    def ccopy(p):
        return remote(code_s, code_r.at[p], c_ss.at[p - 1], c_rs.at[p - 1], away(p))

    def xcopy(k, p):
        return remote(
            xsend.at[k, p - 1], xrecv.at[k, p], x_ss.at[k, p - 1], x_rs.at[k, p - 1], away(p)
        )

    def select(k):
        for i in range(NY + 1):
            if i == 0:
                rows = dot(sel[0, :, toks : 2 * toks], tokbuf[k, 0])
            elif i == NY:
                rows = dot(sel[NY, :, 0:toks], tokbuf[k, NY - 1])
            else:
                rows = dot(sel[i], tokbuf[k, i - 1 : i + 1].reshape(2 * toks, width))
            rows = rows.astype(BF16).reshape(PEERS, TILE, width)
            xrecv[k, 0, i * TILE : (i + 1) * TILE] = rows[0]
            xsend[k, :, i * TILE : (i + 1) * TILE] = rows[1:]

    order = [4, 5, 2, 3, 6, 7, 1]

    def accumulate(k):
        col = chunk_column(k, z)
        for p in range(1, PEERS):
            xcopy(k, p).wait_recv()

        def group(g, _):
            rows = xrecv[k, pl.ds(g * GROUP, GROUP)].reshape(GROUP * block, width)
            weight = winb[col]
            factor = finb[:, col].reshape(8 * rank, width)
            pre[g, :, 0 : 2 * hidden] += dot(rows, weight)
            pre[g, :, 2 * hidden :] += dot(rows, factor, ((1,), (1,)))
            return 0

        lax.fori_loop(0, PEERS // GROUP, group, 0)

    zsend(0, 1)
    zsend(1, 1)
    pre[...] = jnp.zeros_like(pre)

    def slot_a(t, _):
        for h in range(4, 0, -1):
            k = t - h

            @pl.when((k >= 0) & (k < CHUNKS))
            def _():
                for d in range(2):
                    ycopy(k, h, d).wait_recv()
                    if h < 4:
                        ycopy(k, h + 1, d).start()

            @pl.when(k == 0)
            def _():
                for d in hops_of_meta(h):
                    mcopy(h, d).wait_recv()
                if h < 4:
                    for d in hops_of_meta(h + 1):
                        mcopy(h + 1, d).start()

        @pl.when(t == 0)
        def _():
            for d in range(2):
                mcopy(1, d).start()

        @pl.when(t < CHUNKS)
        def _():
            for d in range(2):
                ycopy(t, 1, d).start()

        for h in range(0, 5):

            @pl.when(t == h)
            def _():
                for q in range(max(0, 2 * h - 1), min(2 * h, 7) + 1):
                    build(q)

        @pl.when(t == 4)
        def _():
            tenants()
            for p in order:
                ccopy(p).start()

        @pl.when((t >= 4) & (t < CHUNKS + 4))
        def _():
            k = t - 4
            select(k)
            for p in order:
                xcopy(k, p).start()

        for h in range(1, 5):

            @pl.when(t == h)
            def _():
                for kind in (0, 1):
                    zarrive(kind, h)
                    if h < 4:
                        zsend(kind, h + 1)
                if h == 1:
                    zsend(2, 1)

            @pl.when(t == Z_IN[h - 1])
            def _():
                zarrive(2, h)
                if h < 4:
                    zsend(2, h + 1)
                else:
                    zsend(3, 1)

        for h in range(1, 4):

            @pl.when(t == Z_OUT[h - 1])
            def _():
                zarrive(3, h)
                zsend(3, h + 1)

        @pl.when(t >= 5)
        def _():
            accumulate(t - 5)

        return 0

    lax.fori_loop(0, CHUNKS + 5, slot_a, 0)

    for u in range(8):
        r = u * rank
        wide[r : r + rank // 2, 0:hidden] = fupb[u, 0 : rank // 2]
        wide[r : r + rank // 2, hidden:] = jnp.zeros((rank // 2, hidden), BF16)
        wide[r + rank // 2 : r + rank, 0:hidden] = jnp.zeros((rank // 2, hidden), BF16)
        wide[r + rank // 2 : r + rank, hidden:] = fupb[u, rank // 2 :]
    for p in range(1, PEERS):
        ccopy(p).wait_recv()

    def activate(p, _):
        g, b = p // GROUP, (p % GROUP) * block
        rows = pl.ds(pl.multiple_of(b, block), block)
        codes = code_r[p].astype(F32)
        lane = lax.broadcasted_iota(jnp.int32, (TILE, PEERS * TILE), 1)
        mine = lane == p * TILE + lax.broadcasted_iota(jnp.int32, (TILE, PEERS * TILE), 0)
        column = jnp.concatenate(
            [
                jnp.sum(jnp.where(mine, codes[i : i + 1, :], 0.0), axis=1, keepdims=True)
                for i in range(NY + 1)
            ],
            axis=0,
        )
        of_lane = (lax.broadcasted_iota(jnp.int32, (block, 8 * rank), 1) // rank).astype(F32)
        keep = jnp.where(column == of_lane, adp_ref[...], 0.0)
        low = (pre[g, rows, 2 * hidden :] * keep).astype(BF16)
        total = pre[g, rows, 0 : 2 * hidden] + dot(low, wide[...])
        gate, up = total[:, :hidden], total[:, hidden:]
        act[g, rows] = (gate / (1.0 + jnp.exp(-gate)) * up).astype(BF16)
        return 0

    lax.fori_loop(0, PEERS, activate, 0)

    def sent(k, _):
        for p in range(1, PEERS):
            xcopy(k, p).wait_send()
        for h in range(1, 5):
            for d in range(2):
                ycopy(k, h, d).wait_send()
        return 0

    lax.fori_loop(0, CHUNKS, sent, 0)
    for p in range(1, PEERS):
        ccopy(p).wait_send()
    for h in range(1, 5):
        for d in hops_of_meta(h):
            mcopy(h, d).wait_send()
    zarrive(3, 4)

    def bcopy(k, p):
        return remote(
            xsend.at[k, p - 1], xret.at[k, p], b_ss.at[k, p - 1], b_rs.at[k, p - 1], back(p)
        )

    def rcopy(k, h, d):
        src, dst = rs_s.at[k, h - 1, d], rs_r.at[k, h - 1, d]
        if h == 4:
            src, dst = src.at[pl.ds(d * half, half)], dst.at[pl.ds(d * half, half)]
        return remote(src, dst, r_ss.at[k, h - 1, d], r_rs.at[k, h - 1, d], ring[1 - d])

    def down(k):
        col = chunk_column(k, z)
        for g in (1, 0):
            rows = dot(act[g], woutb[col]).astype(BF16).reshape(GROUP, block, width)
            if g == 0:
                xret[k, 0] = rows[0]
                xsend[k, 0 : GROUP - 1] = rows[1:]
            else:
                xsend[k, GROUP - 1 : 2 * GROUP - 1] = rows
            for p in order:
                if p // GROUP == g:
                    bcopy(k, p).start()

    def combine(k):
        for p in range(1, PEERS):
            bcopy(k, p).wait_recv()
        for q in range(NY - 1, -1, -1):
            rows = xret[k, :, q * TILE : (q + 2) * TILE].reshape(256, width)
            both = dot(mix[q], rows)
            total = both[:toks] + both[toks:]
            if q == NY - 1:
                for d in range(2):
                    rs_s[k, 3, d, d * half : (d + 1) * half] = total[d * half : (d + 1) * half].astype(BF16)
                    rcopy(k, 4, d).start()
            else:
                part[k, q] = total

    def slot_b(t, _):
        for h in range(1, 5):
            k = t - 1 - (5 - h)

            @pl.when((k >= 0) & (k < CHUNKS))
            def _():
                for d in range(2):
                    rcopy(k, h, d).wait_recv()
                    if h == 1:
                        continue
                    q = place_of(h - 1, d)
                    span = slice(d * half, (d + 1) * half)
                    if h == 4:
                        rest = slice((1 - d) * half, (2 - d) * half)
                        rs_s[k, h - 2, d, rest] = part[k, q, rest].astype(BF16)
                    else:
                        span = slice(0, toks)
                    rs_s[k, h - 2, d, span] = (
                        part[k, q, span] + rs_r[k, h - 1, d, span].astype(F32)
                    ).astype(BF16)
                    rcopy(k, h - 1, d).start()
                if h == 1:
                    total = part[k, 0] + rs_r[k, 0, 0].astype(F32) + rs_r[k, 0, 1].astype(F32)
                    col = pl.multiple_of(chunk_column(k, z) * width, width)
                    out_ref[:, pl.ds(col, width)] = total.astype(BF16)

        @pl.when(t < CHUNKS)
        def _():
            down(t)

        @pl.when((t >= 1) & (t < CHUNKS + 1))
        def _():
            combine(t - 1)

        return 0

    lax.fori_loop(0, CHUNKS + 5, slot_b, 0)

    def drained(k, _):
        for p in range(1, PEERS):
            bcopy(k, p).wait_send()
        for h in range(1, 5):
            for d in range(2):
                rcopy(k, h, d).wait_send()
        return 0

    lax.fori_loop(0, CHUNKS, drained, 0)
    for kind in range(4):
        for h in range(1, 5):
            zsent(kind, h)


Z_IN = (3, 5, 7, 8)
Z_OUT = (9, 10, 11)


def shards(
    tokens,
    chosen_expert_index,
    router_weight_logits,
    token_tenant_index,
    adapted,
    gate_up_weight,
    down_weight,
    adapter_input_factors,
    adapter_output_factors,
):
    toks, model = tokens.shape
    width = model // CHUNKS
    hidden = down_weight.shape[1]
    rank = adapter_input_factors.shape[2]
    block = NY * SLOTS
    kept = jnp.repeat(adapted[:, 0].astype(F32), rank)[None, :]
    vmem = pl.BlockSpec(memory_space=pltpu.VMEM)
    dma = pltpu.SemaphoreType.DMA
    return pl.pallas_call(
        layer_kernel,
        out_shape=jax.ShapeDtypeStruct((toks, model), BF16),
        in_specs=[vmem] * 9,
        out_specs=vmem,
        scratch_shapes=[
            pltpu.VMEM((CHUNKS, NY, toks, width), BF16),
            pltpu.VMEM((NY, 24, toks), F32),
            pltpu.VMEM((NY + 1, PEERS * TILE, 2 * toks), BF16),
            pltpu.VMEM((NY, 2 * toks, 256), BF16),
            pltpu.VMEM((CHUNKS, PEERS - 1, block, width), BF16),
            pltpu.VMEM((CHUNKS, PEERS, block, width), BF16),
            pltpu.VMEM((TILE, PEERS * TILE), BF16),
            pltpu.VMEM((PEERS, TILE, PEERS * TILE), BF16),
            pltpu.VMEM((8, width, 2 * hidden), BF16),
            pltpu.VMEM((8, hidden, width), BF16),
            pltpu.VMEM((8, CHUNKS, rank, width), BF16),
            pltpu.VMEM((8, rank, hidden), BF16),
            pltpu.VMEM((8 * rank, 2 * hidden), BF16),
            pltpu.VMEM((PEERS // GROUP, GROUP * block, 2 * hidden + 8 * rank), F32),
            pltpu.VMEM((PEERS // GROUP, GROUP * block, hidden), BF16),
            pltpu.VMEM((CHUNKS, PEERS, block, width), BF16),
            pltpu.VMEM((CHUNKS, NY - 1, toks, width), F32),
            pltpu.VMEM((CHUNKS, 4, 2, toks, width), BF16),
            pltpu.VMEM((CHUNKS, 4, 2, toks, width), BF16),
            dma((CHUNKS, 4, 2)),
            dma((CHUNKS, 4, 2)),
            dma((4, 2)),
            dma((4, 2)),
            dma((CHUNKS, PEERS - 1)),
            dma((CHUNKS, PEERS - 1)),
            dma((PEERS - 1,)),
            dma((PEERS - 1,)),
            dma((4, 4, 2)),
            dma((4, 4, 2)),
            dma((CHUNKS, PEERS - 1)),
            dma((CHUNKS, PEERS - 1)),
            dma((CHUNKS, 4, 2)),
            dma((CHUNKS, 4, 2)),
        ],
        compiler_params=pltpu.CompilerParams(
            collective_id=0, has_side_effects=True, vmem_limit_bytes=60 * 1024 * 1024
        ),
        cost_estimate=pl.CostEstimate(flops=8 * 10**9, bytes_accessed=3 * 10**6, transcendentals=0),
    )(
        tokens,
        chosen_expert_index.T,
        router_weight_logits.T,
        token_tenant_index[None, :],
        kept,
        gate_up_weight[0],
        down_weight[0],
        adapter_input_factors[0, 0],
        adapter_output_factors[0, 0],
    )


def solution(mesh):
    placed = (
        P(("expert", "store"), None),
        P(("expert", "store"), None),
        P(("expert", "store"), None),
        P(("expert", "store")),
        P(None, "expert"),
        P("expert", "store", None),
        P("expert", None, "store"),
        P("store", "expert", None, None),
        P("store", "expert", None, None),
    )
    return jax.shard_map(
        shards, mesh=mesh, in_specs=placed, out_specs=P(("expert", "store"), None), check_vma=False
    )
```

```python
import jax
import jax.numpy as jnp
from jax import lax
from jax.experimental import pallas as pl
from jax.experimental.pallas import tpu as pltpu
from jax.sharding import PartitionSpec as P

MESH = pl.DeviceIdType.MESH
NX, NY, NC = 4, 8, 2
PEERS = NX * NC
SLOTS = 18
TILE = 16
CHUNKS = 8
GROUP = 4
LAG = 2
F32, BF16 = jnp.float32, jnp.bfloat16


def dot(a, b, dims=((1,), (0,))):
    return lax.dot_general(a, b, (dims, ((), ())), preferred_element_type=F32)


def chunk_column(step, z):
    far = (step + 1) // 2
    return jnp.where(step % 2 == 1, z - far + 8, z + far) % 8


def layer_kernel(
    tok_ref, idx_ref, logit_ref, ten_ref, adp_ref, win_ref, wout_ref, fin_ref, fup_ref, out_ref,
    tokbuf, meta, sel, mix, xsend, xrecv, code_s, code_r, winb, woutb, finb, fupb, wide, pre, act,
    xret, own, rs_s, rs_r,
    y_ss, y_rs, m_ss, m_rs, x_ss, x_rs, c_ss, c_rs, w_ss, w_rs, b_ss, b_rs, r_ss, r_rs,
):
    toks = tok_ref.shape[0]
    topk = idx_ref.shape[0]
    width = tok_ref.shape[1] // CHUNKS
    hidden = wout_ref.shape[0]
    rank = fin_ref.shape[0]
    block = NY * SLOTS
    half = toks // 2
    e = lax.axis_index("expert")
    z = lax.axis_index("store")
    x, y, c = e // (NY * NC), (e // NC) % NY, e % NC

    def at(dx, dy, dc):
        return (((x + dx) % NX * NY + (y + dy) % NY) * NC + (c + dc) % NC, z)

    def away(p):
        return at(p // NC, 0, p % NC)

    def back(p):
        return at(NX - p // NC, 0, p % NC)

    ring = (at(0, 1, 0), at(0, NY - 1, 0))
    zring = ((e, (z + 1) % 8), (e, (z + 7) % 8))

    def remote(src, dst, ss, rs, dev):
        return pltpu.make_async_remote_copy(
            src_ref=src, dst_ref=dst, send_sem=ss, recv_sem=rs, device_id=dev, device_id_type=MESH
        )

    def await_bytes(ref, sem):
        pltpu.make_async_copy(ref, ref, sem).wait()

    barrier = pltpu.get_barrier_semaphore()
    partners = [*ring, *zring] + [away(p) for p in range(1, PEERS)]
    for dev in partners:
        pl.semaphore_signal(barrier, inc=1, device_id=dev, device_id_type=MESH)

    winb[z] = win_ref[...]
    woutb[z] = wout_ref[...]
    fupb[z] = fup_ref[...]
    for k in range(CHUNKS):
        finb[z, k] = fin_ref[:, k * width : (k + 1) * width]

    def take(k, _):
        col = pl.multiple_of(chunk_column(k, z) * width, width)
        tokbuf[k, 0] = tok_ref[:, pl.ds(col, width)]
        return 0

    lax.fori_loop(0, CHUNKS, take, 0)

    ids = idx_ref[...]
    experts = NX * NY * NC
    named = lax.broadcasted_iota(jnp.int32, (experts, toks), 0)
    chosen = jnp.zeros((experts, toks), F32)
    for k in range(topk):
        chosen = chosen + jnp.where(ids[k : k + 1, :] == named, 1.0, 0.0)
    before = jnp.where(
        lax.broadcasted_iota(jnp.int32, (toks, toks), 0)
        < lax.broadcasted_iota(jnp.int32, (toks, toks), 1),
        1.0,
        0.0,
    ).astype(BF16)
    rank_of = dot(chosen.astype(BF16), before)
    peer = (((ids // (NY * NC)) - x + NX) % NX) * NC + (ids % NC + c) % NC
    place = ((ids // NC) % NY * 256 + peer * 32).astype(F32)
    for k in range(topk):
        slot = jnp.sum(jnp.where(ids[k : k + 1, :] == named, rank_of, 0.0), axis=0, keepdims=True)
        meta[0, k : k + 1, :] = place[k : k + 1, :] + slot
    logits = logit_ref[...]
    meta[0, topk : 2 * topk, :] = logits / jnp.sum(logits, axis=0, keepdims=True)
    meta[0, 2 * topk : 3 * topk, :] = jnp.broadcast_to(ten_ref[...], (topk, toks)).astype(F32)

    pl.semaphore_wait(barrier, len(partners))

    kinds = (finb, fupb, winb, woutb)
    FIN, FUP, WIN, WOUT = range(4)

    def zsend(kind, h):
        for d in range(2):
            ref = kinds[kind].at[(z - (h - 1) + 8) % 8 if d == 0 else (z + (h - 1)) % 8]
            if h == 4:
                n = ref.shape[0] // 2
                ref = ref.at[pl.ds(d * n, n)]
            remote(ref, ref, w_ss.at[kind], w_rs.at[kind, h - 1], zring[d]).start()

    def zarrive(kind, h):
        await_bytes(kinds[kind].at[pl.ds(0, 1 if h == 4 else 2)], w_rs.at[kind, h - 1])

    def place_of(h, d):
        return 0 if h == 0 else (7 if h == 4 else 2 * h - 1 + d)

    def ysend(k, h):
        for d in range(2):
            src, dst = tokbuf.at[k, place_of(h - 1, d)], tokbuf.at[k, place_of(h, d)]
            if h == 4:
                src, dst = src.at[pl.ds(d * half, half)], dst.at[pl.ds(d * half, half)]
            remote(src, dst, y_ss.at[h // 4], y_rs.at[k, h - 1], ring[d]).start()

    def yarrive(k, h):
        await_bytes(tokbuf.at[k, pl.ds(0, 1 if h == 4 else 2)], y_rs.at[k, h - 1])

    def msend(h):
        for d in range(1 if h == 4 else 2):
            remote(meta.at[place_of(h - 1, d)], meta.at[place_of(h, d)], m_ss, m_rs.at[h - 1], ring[d]).start()

    def marrive(h):
        await_bytes(meta.at[pl.ds(0, 1 if h == 4 else 2)], m_rs.at[h - 1])

    row_no = lax.broadcasted_iota(jnp.int32, (256, toks), 0)

    def build(q):
        want = (row_no + (y * 256 - 2 * q)).astype(F32)
        hot = jnp.zeros((256, toks), F32)
        share = jnp.zeros((256, toks), F32)
        for k in range(topk):
            same = meta[q, k : k + 1, :] == want
            hot = jnp.where(same, 1.0, hot)
            share = jnp.where(same, meta[q, topk + k : topk + k + 1, :], share)
        hot = hot.astype(BF16).reshape(PEERS, 2, TILE, toks)
        sel[q, :, toks : 2 * toks] = hot[:, 0].reshape(PEERS * TILE, toks)
        sel[q + 1, :, 0:toks] = hot[:, 1].reshape(PEERS * TILE, toks)
        share = share.T
        high = share.astype(BF16)
        mix[q, 0:toks] = high
        mix[q, toks : 2 * toks] = (share - high.astype(F32)).astype(BF16)

    def tenants():
        lane_of = lax.broadcasted_iota(jnp.int32, (TILE, toks), 0)
        codes = jnp.zeros((TILE, PEERS * TILE), F32)
        for i in range(NY + 1):
            mine = lane_of == i
            if i > 0:
                v = jnp.where(mine, meta[i - 1, 2 * topk : 2 * topk + 1, :], 0.0).astype(BF16)
                codes = codes + dot(v, sel[i, :, 0:toks], ((1,), (1,)))
            if i < NY:
                v = jnp.where(mine, meta[i, 2 * topk : 2 * topk + 1, :], 0.0).astype(BF16)
                codes = codes + dot(v, sel[i, :, toks : 2 * toks], ((1,), (1,)))
        code_s[...] = codes.astype(BF16)
        code_r[0] = codes.astype(BF16)

    order = [4, 5, 2, 3, 6, 7, 1]
    tiles = {h: (0 if h == 1 else 2 * h - 1, 2 * h + 1) for h in range(1, 5)}

    def rows_of(h):
        return pl.ds(tiles[h][0] * TILE, (tiles[h][1] - tiles[h][0]) * TILE)

    def select(k, h):
        for i in range(*tiles[h]):
            if i == 0:
                rows = dot(sel[0, :, toks : 2 * toks], tokbuf[k, 0])
            elif i == NY:
                rows = dot(sel[NY, :, 0:toks], tokbuf[k, NY - 1])
            else:
                rows = dot(sel[i], tokbuf[k, i - 1 : i + 1].reshape(2 * toks, width))
            rows = rows.astype(BF16).reshape(PEERS, TILE, width)
            xrecv[k, 0, i * TILE : (i + 1) * TILE] = rows[0]
            xsend[k, 1:, i * TILE : (i + 1) * TILE] = rows[1:]
        for p in order:
            remote(
                xsend.at[k, p, rows_of(h)], xrecv.at[k, p, rows_of(h)], x_ss, x_rs.at[k], away(p)
            ).start()

    def xarrive(k):
        await_bytes(xrecv.at[k, pl.ds(1, PEERS - 1)], x_rs.at[k])

    def block_rows(k, g):
        return xrecv[k, pl.ds(g * GROUP, GROUP)].reshape(GROUP * block, width)

    def accumulate(k, g):
        pre[g, :, 0 : 2 * hidden] += dot(block_rows(k, g), winb[chunk_column(k, z)])

    def lower(k, g):
        factor = finb[:, chunk_column(k, z)].reshape(8 * rank, width)
        pre[g, :, 2 * hidden :] += dot(block_rows(k, g), factor, ((1,), (1,)))

    def lower_of(first, last):
        def step(i, _):
            lower(i // 2, i % 2)
            return 0

        lax.fori_loop(2 * first, 2 * last, step, 0)

    for kind in (WIN, FIN, FUP):
        zsend(kind, 1)
    pre[...] = jnp.zeros_like(pre)

    def slot_a(t, _):
        for h in range(4, 0, -1):
            k = t - h

            @pl.when((k >= 0) & (k < CHUNKS))
            def _():
                yarrive(k, h)
                if h < 4:
                    ysend(k, h + 1)

            @pl.when(k == 0)
            def _():
                marrive(h)
                if h < 4:
                    msend(h + 1)

        @pl.when(t == 0)
        def _():
            msend(1)

        @pl.when(t < CHUNKS)
        def _():
            ysend(t, 1)

        for h in range(0, 5):

            @pl.when(t == h)
            def _():
                for q in range(max(0, 2 * h - 1), min(2 * h, 7) + 1):
                    build(q)

        for h in range(4, 0, -1):
            k = t - h

            @pl.when((k >= 0) & (k < CHUNKS))
            def _():
                select(k, h)

        @pl.when(t == 4)
        def _():
            tenants()
            for p in order:
                remote(code_s, code_r.at[p], c_ss, c_rs, away(p)).start()
            for kind in (WIN, FIN, FUP):
                zarrive(kind, 1)
                zsend(kind, 2)

        @pl.when(t == 6)
        def _():
            zarrive(WIN, 2)
            zsend(WIN, 3)

        @pl.when(t == 7)
        def _():
            for kind in (FIN, FUP):
                zarrive(kind, 2)
                zsend(kind, 3)

        @pl.when(t == 8)
        def _():
            zarrive(WIN, 3)
            zsend(WIN, 4)

        @pl.when(t == 9)
        def _():
            for kind in (FIN, FUP):
                zarrive(kind, 3)
                zsend(kind, 4)

        @pl.when(t == 10)
        def _():
            zarrive(WIN, 4)
            zsend(WOUT, 1)
            for kind in (FIN, FUP):
                zarrive(kind, 4)
            lower_of(0, 4)

        @pl.when(t == 11)
        def _():
            lower_of(4, 6)

        @pl.when(t >= 5)
        def _():
            xarrive(t - 5)

            def group(g, _):
                accumulate(t - 5, g)
                return 0

            lax.fori_loop(0, PEERS // GROUP, group, 0)

        return 0

    lax.fori_loop(0, CHUNKS + 4, slot_a, 0)

    for u in range(8):
        r = u * rank
        wide[r : r + rank // 2, 0:hidden] = fupb[u, 0 : rank // 2]
        wide[r : r + rank // 2, hidden:] = jnp.zeros((rank // 2, hidden), BF16)
        wide[r + rank // 2 : r + rank, 0:hidden] = jnp.zeros((rank // 2, hidden), BF16)
        wide[r + rank // 2 : r + rank, hidden:] = fupb[u, rank // 2 :]
    lower_of(6, 7)
    await_bytes(code_r.at[pl.ds(1, PEERS - 1)], c_rs)
    lane_rank = lax.broadcasted_iota(jnp.int32, (1, 8 * rank), 1) // rank
    adapted = jnp.zeros((1, 8 * rank), F32)
    for u in range(8):
        adapted = jnp.where(lane_rank == u, adp_ref[0, u].astype(F32), adapted)

    def activate(p):
        g, b = p // GROUP, (p % GROUP) * block
        rows = pl.ds(pl.multiple_of(b, block), block)
        codes = code_r[p].astype(F32)
        lane = lax.broadcasted_iota(jnp.int32, (TILE, PEERS * TILE), 1)
        mine = lane == p * TILE + lax.broadcasted_iota(jnp.int32, (TILE, PEERS * TILE), 0)
        column = jnp.concatenate(
            [
                jnp.sum(jnp.where(mine, codes[i : i + 1, :], 0.0), axis=1, keepdims=True)
                for i in range(NY + 1)
            ],
            axis=0,
        )
        of_lane = (lax.broadcasted_iota(jnp.int32, (block, 8 * rank), 1) // rank).astype(F32)
        keep = jnp.where(column == of_lane, adapted, 0.0)
        low = (pre[g, rows, 2 * hidden :] * keep).astype(BF16)
        total = pre[g, rows, 0 : 2 * hidden] + dot(low, wide[...])
        gate, up = total[:, :hidden], total[:, hidden:]
        act[g, rows] = (gate / (1.0 + jnp.exp(-gate)) * up).astype(BF16)

    await_bytes(xsend.at[:, pl.ds(1, PEERS - 1)], x_ss)

    def send_back(k, h, p):
        remote(
            xsend.at[k, p, rows_of(h)], xret.at[k, p, rows_of(h)], b_ss, b_rs.at[k, h - 1], back(p)
        ).start()

    def returned(k, h):
        await_bytes(xret.at[k, pl.ds(1, PEERS - 1), rows_of(h)], b_rs.at[k, h - 1])

    def rsend(k, h, d):
        src, dst = rs_s.at[k, h - 1, d], rs_r.at[k, h - 1, d]
        if h == 4:
            src, dst = src.at[pl.ds(d * half, half)], dst.at[pl.ds(d * half, half)]
        remote(src, dst, r_ss.at[h // 4], r_rs.at[k, h - 1], ring[1 - d]).start()

    def rarrive(k, h):
        await_bytes(rs_r.at[k, h - 1, pl.ds(0, 1 if h == 4 else 2)], r_rs.at[k, h - 1])

    def down(k, g):
        rows = dot(act[g], woutb[chunk_column(k, z)]).astype(BF16).reshape(GROUP, block, width)
        xsend[k, pl.ds(g * GROUP, GROUP)] = rows

        @pl.when(g == 0)
        def _():
            xret[k, 0] = rows[0]

    xarrive(CHUNKS - 1)

    def turn(i, _):
        g = 1 - i
        accumulate(CHUNKS - 1, g)
        lower(CHUNKS - 1, g)

        def one(p, _):
            activate(g * GROUP + p)
            return 0

        lax.fori_loop(0, GROUP, one, 0)
        down(0, g)
        for here in range(2):

            @pl.when(g == here)
            def _():
                for p in order:
                    if p // GROUP == here:
                        send_back(0, 4, p)

        return 0

    lax.fori_loop(0, 2, turn, 0)

    def mixed(k, q):
        rows = xret[k, :, q * TILE : (q + 2) * TILE].reshape(256, width)
        both = dot(mix[q], rows)
        return both[:toks] + both[toks:]

    def combine(k, h):
        returned(k, h)
        if h == 4:
            total = mixed(k, 7)
            for d in range(2):
                span = slice(d * half, (d + 1) * half)
                rs_s[k, 3, d, span] = total[span].astype(BF16)
                rsend(k, 4, d)
            return
        rarrive(k, h + 1)
        for d in range(2):
            total = mixed(k, place_of(h, d))
            if h == 3:
                span, rest = slice(d * half, (d + 1) * half), slice((1 - d) * half, (2 - d) * half)
                rs_s[k, 2, d, rest] = total[rest].astype(BF16)
                rs_s[k, 2, d, span] = (total[span] + rs_r[k, 3, d, span].astype(F32)).astype(BF16)
            else:
                rs_s[k, h - 1, d] = (total + rs_r[k, h, d].astype(F32)).astype(BF16)
            rsend(k, h, d)
        if h == 1:
            own[k] = mixed(k, 0)

    def finish(k):
        rarrive(k, 1)
        total = own[k] + rs_r[k, 0, 0].astype(F32) + rs_r[k, 0, 1].astype(F32)
        col = pl.multiple_of(chunk_column(k, z) * width, width)
        out_ref[:, pl.ds(col, width)] = total.astype(BF16)

    def slot_b(t, _):
        for h in range(1, 5):

            @pl.when(t == 2 * h - 2)
            def _():
                zarrive(WOUT, h)
                if h < 4:
                    zsend(WOUT, h + 1)

        @pl.when((t >= 1) & (t < CHUNKS))
        def _():
            def group(g, _):
                down(t, g)
                return 0

            lax.fori_loop(0, PEERS // GROUP, group, 0)
            for p in order:
                send_back(t, 4, p)

        for h in range(3, 0, -1):
            k = t - (4 - h)

            @pl.when((k >= 0) & (k < CHUNKS))
            def _():
                for p in order:
                    send_back(k, h, p)

        done = t - LAG - 4

        @pl.when(done >= 0)
        def _():
            finish(done)

        for h in range(1, 5):
            k = t - LAG - (4 - h)

            @pl.when((k >= 0) & (k < CHUNKS))
            def _():
                combine(k, h)

        return 0

    lax.fori_loop(0, CHUNKS + LAG + 4, slot_b, 0)

    await_bytes(xsend.at[:, pl.ds(1, PEERS - 1)], b_ss)
    await_bytes(tokbuf.at[:, pl.ds(0, 6)], y_ss.at[0])
    await_bytes(tokbuf.at[:, 7], y_ss.at[1])
    await_bytes(rs_s.at[:, pl.ds(0, 3)], r_ss.at[0])
    await_bytes(rs_s.at[:, 3, 0], r_ss.at[1])
    await_bytes(meta.at[pl.ds(0, 7)], m_ss)
    await_bytes(code_r.at[pl.ds(1, PEERS - 1)], c_ss)
    for kind in range(4):
        await_bytes(kinds[kind].at[pl.ds(0, 7)], w_ss.at[kind])


def shards(
    tokens,
    chosen_expert_index,
    router_weight_logits,
    token_tenant_index,
    adapted,
    gate_up_weight,
    down_weight,
    adapter_input_factors,
    adapter_output_factors,
):
    toks, model = tokens.shape
    width = model // CHUNKS
    hidden = down_weight.shape[1]
    rank = adapter_input_factors.shape[2]
    block = NY * SLOTS
    vmem = pl.BlockSpec(memory_space=pltpu.VMEM)
    dma = pltpu.SemaphoreType.DMA
    return pl.pallas_call(
        layer_kernel,
        out_shape=jax.ShapeDtypeStruct((toks, model), BF16),
        in_specs=[vmem] * 4 + [pl.BlockSpec(memory_space=pltpu.SMEM)] + [vmem] * 4,
        out_specs=vmem,
        scratch_shapes=[
            pltpu.VMEM((CHUNKS, NY, toks, width), BF16),
            pltpu.VMEM((NY, 24, toks), F32),
            pltpu.VMEM((NY + 1, PEERS * TILE, 2 * toks), BF16),
            pltpu.VMEM((NY, 2 * toks, 256), BF16),
            pltpu.VMEM((CHUNKS, PEERS, block, width), BF16),
            pltpu.VMEM((CHUNKS, PEERS, block, width), BF16),
            pltpu.VMEM((TILE, PEERS * TILE), BF16),
            pltpu.VMEM((PEERS, TILE, PEERS * TILE), BF16),
            pltpu.VMEM((8, width, 2 * hidden), BF16),
            pltpu.VMEM((8, hidden, width), BF16),
            pltpu.VMEM((8, CHUNKS, rank, width), BF16),
            pltpu.VMEM((8, rank, hidden), BF16),
            pltpu.VMEM((8 * rank, 2 * hidden), BF16),
            pltpu.VMEM((PEERS // GROUP, GROUP * block, 2 * hidden + 8 * rank), F32),
            pltpu.VMEM((PEERS // GROUP, GROUP * block, hidden), BF16),
            pltpu.VMEM((CHUNKS, PEERS, block, width), BF16),
            pltpu.VMEM((CHUNKS, toks, width), F32),
            pltpu.VMEM((CHUNKS, 4, 2, toks, width), BF16),
            pltpu.VMEM((CHUNKS, 4, 2, toks, width), BF16),
            dma((2,)),
            dma((CHUNKS, 4)),
            dma,
            dma((4,)),
            dma,
            dma((CHUNKS,)),
            dma,
            dma,
            dma((4,)),
            dma((4, 4)),
            dma,
            dma((CHUNKS, 4)),
            dma((2,)),
            dma((CHUNKS, 4)),
        ],
        compiler_params=pltpu.CompilerParams(
            collective_id=0, has_side_effects=True, vmem_limit_bytes=60 * 1024 * 1024
        ),
        cost_estimate=pl.CostEstimate(flops=8 * 10**9, bytes_accessed=3 * 10**6, transcendentals=0),
    )(
        tokens,
        chosen_expert_index.T,
        router_weight_logits.T,
        token_tenant_index[None, :],
        adapted.T,
        gate_up_weight[0],
        down_weight[0],
        adapter_input_factors[0, 0],
        adapter_output_factors[0, 0],
    )


def solution(mesh):
    placed = (
        P(("expert", "store"), None),
        P(("expert", "store"), None),
        P(("expert", "store"), None),
        P(("expert", "store")),
        P(None, "expert"),
        P("expert", "store", None),
        P("expert", None, "store"),
        P("store", "expert", None, None),
        P("store", "expert", None, None),
    )
    return jax.shard_map(
        shards, mesh=mesh, in_specs=placed, out_specs=P(("expert", "store"), None), check_vma=False
    )
```

```python
import jax
import jax.numpy as jnp
from jax import lax
from jax.experimental import pallas as pl
from jax.experimental.pallas import tpu as pltpu
from jax.sharding import PartitionSpec as P

MESH = pl.DeviceIdType.MESH
FIN, FUP, WIN, WOUT = range(4)
NX, NY, NC = 4, 8, 2
PEERS = NX * NC
SLOTS = 18
TILE = 16
CHUNKS = 8
GROUP = 4
LAG = 2
HOP = 2
STAGGER = 1
LAST_A = CHUNKS + 4 * HOP
LAST_B = CHUNKS - 1 + LAG + 4 * HOP
OWN_BACK = CHUNKS + 3 * STAGGER
PLAN_A = (
    (6, ((WIN, 1), (FIN, 1), (FUP, 1)), ((WIN, 2), (FIN, 2), (FUP, 2))),
    (9, ((WIN, 2),), ((WIN, 3),)),
    (10, ((FIN, 2), (FUP, 2)), ((FIN, 3), (FUP, 3))),
    (12, ((WIN, 3), (FIN, 3), (FUP, 3)), ((WIN, 4), (FIN, 4), (FUP, 4))),
    (13, (), ((WOUT, 1),)),
    (14, ((FIN, 4), (FUP, 4)), ()),
)
F32, BF16 = jnp.float32, jnp.bfloat16


def dot(a, b, dims=((1,), (0,))):
    return lax.dot_general(a, b, (dims, ((), ())), preferred_element_type=F32)


def chunk_column(step, z):
    far = (step + 1) // 2
    return jnp.where(step % 2 == 1, z - far + 8, z + far) % 8


def layer_kernel(
    tok_ref, idx_ref, logit_ref, ten_ref, adp_ref, win_ref, wout_ref, fin_ref, fup_ref, out_ref,
    tokbuf, meta, sel, mix, xsend, xrecv, code_s, code_r, winb, woutb, finb, fupb, wide, pre, act,
    xret, rs_s, rs_r,
    y_ss, y_rs, m_ss, m_rs, x_ss, x_rs, c_ss, c_rs, w_ss, w_rs, b_ss, b_rs, r_ss, r_rs,
):
    toks = tok_ref.shape[0]
    topk = idx_ref.shape[0]
    width = tok_ref.shape[1] // CHUNKS
    hidden = wout_ref.shape[0]
    rank = fin_ref.shape[0]
    block = NY * SLOTS
    half = toks // 2
    e = lax.axis_index("expert")
    z = lax.axis_index("store")
    x, y, c = e // (NY * NC), (e // NC) % NY, e % NC

    def at(dx, dy, dc):
        return (((x + dx) % NX * NY + (y + dy) % NY) * NC + (c + dc) % NC, z)

    def away(p):
        return at(p // NC, 0, p % NC)

    def back(p):
        return at(NX - p // NC, 0, p % NC)

    ring = (at(0, 1, 0), at(0, NY - 1, 0))
    zring = ((e, (z + 1) % 8), (e, (z + 7) % 8))

    def remote(src, dst, ss, rs, dev):
        return pltpu.make_async_remote_copy(
            src_ref=src, dst_ref=dst, send_sem=ss, recv_sem=rs, device_id=dev, device_id_type=MESH
        )

    def await_bytes(ref, sem):
        pltpu.make_async_copy(ref, ref, sem).wait()

    barrier = pltpu.get_barrier_semaphore()
    partners = [*ring, *zring] + [away(p) for p in range(1, PEERS)]
    for dev in partners:
        pl.semaphore_signal(barrier, inc=1, device_id=dev, device_id_type=MESH)

    winb[z] = win_ref[...]
    woutb[z] = wout_ref[...]
    fupb[z] = fup_ref[...]
    for k in range(CHUNKS):
        finb[z, k] = fin_ref[:, k * width : (k + 1) * width]

    def take(k, _):
        col = pl.multiple_of(chunk_column(k, z) * width, width)
        tokbuf[k, 0] = tok_ref[:, pl.ds(col, width)]
        return 0

    lax.fori_loop(0, CHUNKS, take, 0)

    ids = idx_ref[...]
    experts = NX * NY * NC
    named = lax.broadcasted_iota(jnp.int32, (experts, toks), 0)
    chosen = jnp.zeros((experts, toks), F32)
    for k in range(topk):
        chosen = chosen + jnp.where(ids[k : k + 1, :] == named, 1.0, 0.0)
    before = jnp.where(
        lax.broadcasted_iota(jnp.int32, (toks, toks), 0)
        < lax.broadcasted_iota(jnp.int32, (toks, toks), 1),
        1.0,
        0.0,
    ).astype(BF16)
    rank_of = dot(chosen.astype(BF16), before)
    peer = (((ids // (NY * NC)) - x + NX) % NX) * NC + (ids % NC + c) % NC
    place = ((ids // NC) % NY * 256 + peer * 32).astype(F32)
    for k in range(topk):
        slot = jnp.sum(jnp.where(ids[k : k + 1, :] == named, rank_of, 0.0), axis=0, keepdims=True)
        meta[0, k : k + 1, :] = place[k : k + 1, :] + slot
    logits = logit_ref[...]
    meta[0, topk : 2 * topk, :] = logits / jnp.sum(logits, axis=0, keepdims=True)
    meta[0, 2 * topk : 3 * topk, :] = jnp.broadcast_to(ten_ref[...], (topk, toks)).astype(F32)

    pl.semaphore_wait(barrier, len(partners))

    kinds = (finb, fupb, winb, woutb)

    def zsend(kind, h):
        for d in range(2):
            ref = kinds[kind].at[(z - (h - 1) + 8) % 8 if d == 0 else (z + (h - 1)) % 8]
            if h == 4:
                n = ref.shape[0] // 2
                ref = ref.at[pl.ds(d * n, n)]
            remote(ref, ref, w_ss.at[kind], w_rs.at[kind, h - 1], zring[d]).start()

    def zarrive(kind, h):
        await_bytes(kinds[kind].at[pl.ds(0, 1 if h == 4 else 2)], w_rs.at[kind, h - 1])

    def place_of(h, d):
        return 0 if h == 0 else (7 if h == 4 else 2 * h - 1 + d)

    def ysend(k, h):
        for d in range(2):
            src, dst = tokbuf.at[k, place_of(h - 1, d)], tokbuf.at[k, place_of(h, d)]
            if h == 4:
                src, dst = src.at[pl.ds(d * half, half)], dst.at[pl.ds(d * half, half)]
            remote(src, dst, y_ss.at[h // 4], y_rs.at[k, h - 1], ring[d]).start()

    def yarrive(k, h):
        await_bytes(tokbuf.at[k, pl.ds(0, 1 if h == 4 else 2)], y_rs.at[k, h - 1])

    def msend(h):
        for d in range(1 if h == 4 else 2):
            remote(meta.at[place_of(h - 1, d)], meta.at[place_of(h, d)], m_ss, m_rs.at[h - 1], ring[d]).start()

    def marrive(h):
        await_bytes(meta.at[pl.ds(0, 1 if h == 4 else 2)], m_rs.at[h - 1])

    row_no = lax.broadcasted_iota(jnp.int32, (256, toks), 0)

    def build(q):
        want = (row_no + (y * 256 - 2 * q)).astype(F32)
        hot = jnp.zeros((256, toks), F32)
        share = jnp.zeros((256, toks), F32)
        for k in range(topk):
            same = meta[q, k : k + 1, :] == want
            hot = jnp.where(same, 1.0, hot)
            share = jnp.where(same, meta[q, topk + k : topk + k + 1, :], share)
        hot = hot.astype(BF16).reshape(PEERS, 2, TILE, toks)
        sel[q, :, toks : 2 * toks] = hot[:, 0].reshape(PEERS * TILE, toks)
        sel[q + 1, :, 0:toks] = hot[:, 1].reshape(PEERS * TILE, toks)
        share = share.T
        high = share.astype(BF16)
        mix[q, 0:toks] = high
        mix[q, toks : 2 * toks] = (share - high.astype(F32)).astype(BF16)

    def tenants():
        lane_of = lax.broadcasted_iota(jnp.int32, (TILE, toks), 0)
        codes = jnp.zeros((TILE, PEERS * TILE), F32)
        for i in range(NY + 1):
            mine = lane_of == i
            if i > 0:
                v = jnp.where(mine, meta[i - 1, 2 * topk : 2 * topk + 1, :], 0.0).astype(BF16)
                codes = codes + dot(v, sel[i, :, 0:toks], ((1,), (1,)))
            if i < NY:
                v = jnp.where(mine, meta[i, 2 * topk : 2 * topk + 1, :], 0.0).astype(BF16)
                codes = codes + dot(v, sel[i, :, toks : 2 * toks], ((1,), (1,)))
        code_s[...] = codes.astype(BF16)
        code_r[0] = codes.astype(BF16)

    order = [4, 5, 2, 3, 6, 7, 1]
    tiles = {h: (max(0, 2 * h - 1), 2 * h + 1) for h in range(0, 5)}

    def rows_of(h):
        return pl.ds(tiles[h][0] * TILE, (tiles[h][1] - tiles[h][0]) * TILE)

    def select(k, h):
        for i in range(*tiles[h]):
            if i == 0:
                rows = dot(sel[0, :, toks : 2 * toks], tokbuf[k, 0])
            elif i == NY:
                rows = dot(sel[NY, :, 0:toks], tokbuf[k, NY - 1])
            else:
                rows = dot(sel[i], tokbuf[k, i - 1 : i + 1].reshape(2 * toks, width))
            rows = rows.astype(BF16).reshape(PEERS, TILE, width)
            xrecv[k, 0, i * TILE : (i + 1) * TILE] = rows[0]
            xsend[k, 1:, i * TILE : (i + 1) * TILE] = rows[1:]
        for p in order:
            remote(
                xsend.at[k, p, rows_of(h)], xrecv.at[k, p, rows_of(h)], x_ss, x_rs.at[k], away(p)
            ).start()

    def xarrive(k):
        await_bytes(xrecv.at[k, pl.ds(1, PEERS - 1)], x_rs.at[k])

    def block_rows(k, g):
        return xrecv[k, pl.ds(g * GROUP, GROUP)].reshape(GROUP * block, width)

    def accumulate(k, g):
        pre[g, :, 0 : 2 * hidden] += dot(block_rows(k, g), winb[chunk_column(k, z)])

    def lower(k, g):
        factor = finb[:, chunk_column(k, z)].reshape(8 * rank, width)
        pre[g, :, 2 * hidden :] += dot(block_rows(k, g), factor, ((1,), (1,)))

    def lower_of(first, last):
        def step(i, _):
            lower(i // 2, i % 2)
            return 0

        lax.fori_loop(2 * first, 2 * last, step, 0)

    for kind in (WIN, FIN, FUP):
        zsend(kind, 1)
    pre[...] = jnp.zeros_like(pre)

    def slot_a(t, _):
        for h in range(4, 0, -1):
            k = t - HOP * h

            @pl.when((k >= 0) & (k < CHUNKS))
            def _():
                yarrive(k, h)
                if h < 4:
                    ysend(k, h + 1)

            @pl.when(k == 0)
            def _():
                marrive(h)
                if h < 4:
                    msend(h + 1)

        @pl.when(t == 0)
        def _():
            msend(1)

        @pl.when(t < CHUNKS)
        def _():
            ysend(t, 1)

        for h in range(0, 5):

            @pl.when(t == HOP * h)
            def _():
                for q in range(max(0, 2 * h - 1), min(2 * h, 7) + 1):
                    build(q)

        for h in range(4, 0, -1):
            k = t - HOP * h

            @pl.when((k >= 0) & (k < CHUNKS))
            def _():
                select(k, h)

        @pl.when(t < CHUNKS // 2)
        def _():
            for i in range(2):
                select(2 * t + i, 0)

        @pl.when(t == 4 * HOP)
        def _():
            tenants()
            for p in order:
                remote(code_s, code_r.at[p], c_ss, c_rs, away(p)).start()

        for slot, came, goes in PLAN_A:

            @pl.when(t == slot)
            def _():
                for kind, h in came:
                    zarrive(kind, h)
                for kind, h in goes:
                    zsend(kind, h)

        @pl.when(t == LAST_A - 2)
        def _():
            lower_of(0, 4)

        @pl.when(t == LAST_A - 1)
        def _():
            lower_of(4, 6)

        done = t - 4 * HOP - 1

        @pl.when(done >= 0)
        def _():
            xarrive(done)

            def group(g, _):
                accumulate(done, g)
                return 0

            lax.fori_loop(0, PEERS // GROUP, group, 0)

        return 0

    lax.fori_loop(0, LAST_A, slot_a, 0)

    for u in range(8):
        r = u * rank
        wide[r : r + rank // 2, 0:hidden] = fupb[u, 0 : rank // 2]
        wide[r : r + rank // 2, hidden:] = jnp.zeros((rank // 2, hidden), BF16)
        wide[r + rank // 2 : r + rank, 0:hidden] = jnp.zeros((rank // 2, hidden), BF16)
        wide[r + rank // 2 : r + rank, hidden:] = fupb[u, rank // 2 :]
    zarrive(WIN, 4)
    lower_of(6, 7)
    zarrive(WOUT, 1)
    zsend(WOUT, 2)
    await_bytes(code_r.at[pl.ds(1, PEERS - 1)], c_rs)
    lane_rank = lax.broadcasted_iota(jnp.int32, (1, 8 * rank), 1) // rank
    adapted = jnp.zeros((1, 8 * rank), F32)
    for u in range(8):
        adapted = jnp.where(lane_rank == u, adp_ref[0, u].astype(F32), adapted)

    def activate(p):
        g, b = p // GROUP, (p % GROUP) * block
        rows = pl.ds(pl.multiple_of(b, block), block)
        codes = code_r[p].astype(F32)
        lane = lax.broadcasted_iota(jnp.int32, (TILE, PEERS * TILE), 1)
        mine = lane == p * TILE + lax.broadcasted_iota(jnp.int32, (TILE, PEERS * TILE), 0)
        column = jnp.concatenate(
            [
                jnp.sum(jnp.where(mine, codes[i : i + 1, :], 0.0), axis=1, keepdims=True)
                for i in range(NY + 1)
            ],
            axis=0,
        )
        of_lane = (lax.broadcasted_iota(jnp.int32, (block, 8 * rank), 1) // rank).astype(F32)
        keep = jnp.where(column == of_lane, adapted, 0.0)
        low = (pre[g, rows, 2 * hidden :] * keep).astype(BF16)
        total = pre[g, rows, 0 : 2 * hidden] + dot(low, wide[...])
        gate, up = total[:, :hidden], total[:, hidden:]
        act[g, rows] = (gate / (1.0 + jnp.exp(-gate)) * up).astype(BF16)

    await_bytes(xsend.at[:, pl.ds(1, PEERS - 1)], x_ss)

    def send_back(k, h, p):
        remote(
            xsend.at[k, p, rows_of(h)], xret.at[k, p, rows_of(h)], b_ss, b_rs.at[k, h], back(p)
        ).start()

    def returned(k, h):
        await_bytes(xret.at[k, pl.ds(1, PEERS - 1), rows_of(h)], b_rs.at[k, h])

    def rsend(k, h, d):
        src, dst = rs_s.at[k, h - 1, d], rs_r.at[k, h - 1, d]
        if h == 4:
            src, dst = src.at[pl.ds(d * half, half)], dst.at[pl.ds(d * half, half)]
        remote(src, dst, r_ss.at[h // 4], r_rs.at[k, h - 1], ring[1 - d]).start()

    def rarrive(k, h):
        await_bytes(rs_r.at[k, h - 1, pl.ds(0, 1 if h == 4 else 2)], r_rs.at[k, h - 1])

    def down(k, g):
        rows = dot(act[g], woutb[chunk_column(k, z)]).astype(BF16).reshape(GROUP, block, width)
        xsend[k, pl.ds(g * GROUP, GROUP)] = rows

        @pl.when(g == 0)
        def _():
            xret[k, 0] = rows[0]

    xarrive(CHUNKS - 1)

    def turn(i, _):
        g = 1 - i
        accumulate(CHUNKS - 1, g)
        lower(CHUNKS - 1, g)

        def one(p, _):
            activate(g * GROUP + p)
            return 0

        lax.fori_loop(0, GROUP, one, 0)
        down(0, g)
        for here in range(2):

            @pl.when(g == here)
            def _():
                for p in order:
                    if p // GROUP == here:
                        send_back(0, 4, p)

        return 0

    lax.fori_loop(0, 2, turn, 0)

    def mixed(k, q):
        rows = xret[k, :, q * TILE : (q + 2) * TILE].reshape(256, width)
        both = dot(mix[q], rows)
        return both[:toks] + both[toks:]

    def combine(k, h):
        returned(k, h)
        if h == 4:
            total = mixed(k, 7)
            for d in range(2):
                span = slice(d * half, (d + 1) * half)
                rs_s[k, 3, d, span] = total[span].astype(BF16)
                rsend(k, 4, d)
            return
        rarrive(k, h + 1)
        for d in range(2):
            total = mixed(k, place_of(h, d))
            if h == 3:
                span, rest = slice(d * half, (d + 1) * half), slice((1 - d) * half, (2 - d) * half)
                rs_s[k, 2, d, rest] = total[rest].astype(BF16)
                rs_s[k, 2, d, span] = (total[span] + rs_r[k, 3, d, span].astype(F32)).astype(BF16)
            else:
                rs_s[k, h - 1, d] = (total + rs_r[k, h, d].astype(F32)).astype(BF16)
            rsend(k, h, d)

    def finish(k):
        rarrive(k, 1)
        returned(k, 0)
        total = mixed(k, 0) + rs_r[k, 0, 0].astype(F32) + rs_r[k, 0, 1].astype(F32)
        col = pl.multiple_of(chunk_column(k, z) * width, width)
        out_ref[:, pl.ds(col, width)] = total.astype(BF16)

    def slot_b(t, _):
        for h in range(2, 5):

            @pl.when(t == 2 * h - 2)
            def _():
                zarrive(WOUT, h)
                if h < 4:
                    zsend(WOUT, h + 1)

        @pl.when((t >= 1) & (t < CHUNKS))
        def _():
            def group(g, _):
                down(t, g)
                return 0

            lax.fori_loop(0, PEERS // GROUP, group, 0)
            for p in order:
                send_back(t, 4, p)

        for h in range(3, 0, -1):
            k = t - STAGGER * (4 - h)

            @pl.when((k >= 0) & (k < CHUNKS))
            def _():
                for p in order:
                    send_back(k, h, p)

        early = t - OWN_BACK

        @pl.when((early >= 0) & (early < CHUNKS // 2))
        def _():
            for i in range(2):
                for p in order:
                    send_back(2 * early + i, 0, p)

        for h in range(1, 5):
            k = t - LAG - HOP * (4 - h)

            @pl.when((k >= 0) & (k < CHUNKS))
            def _():
                combine(k, h)

        done = t - (LAST_B - CHUNKS // 2)

        @pl.when(done >= 0)
        def _():
            finish(2 * done)
            finish(2 * done + 1)

        return 0

    lax.fori_loop(0, LAST_B, slot_b, 0)

    await_bytes(xsend.at[:, pl.ds(1, PEERS - 1)], b_ss)
    await_bytes(tokbuf.at[:, pl.ds(0, 6)], y_ss.at[0])
    await_bytes(tokbuf.at[:, 7], y_ss.at[1])
    await_bytes(rs_s.at[:, pl.ds(0, 3)], r_ss.at[0])
    await_bytes(rs_s.at[:, 3, 0], r_ss.at[1])
    await_bytes(meta.at[pl.ds(0, 7)], m_ss)
    await_bytes(code_r.at[pl.ds(1, PEERS - 1)], c_ss)
    for kind in range(4):
        await_bytes(kinds[kind].at[pl.ds(0, 7)], w_ss.at[kind])


def shards(
    tokens,
    chosen_expert_index,
    router_weight_logits,
    token_tenant_index,
    adapted,
    gate_up_weight,
    down_weight,
    adapter_input_factors,
    adapter_output_factors,
):
    toks, model = tokens.shape
    width = model // CHUNKS
    hidden = down_weight.shape[1]
    rank = adapter_input_factors.shape[2]
    block = NY * SLOTS
    vmem = pl.BlockSpec(memory_space=pltpu.VMEM)
    dma = pltpu.SemaphoreType.DMA
    return pl.pallas_call(
        layer_kernel,
        out_shape=jax.ShapeDtypeStruct((toks, model), BF16),
        in_specs=[vmem] * 4 + [pl.BlockSpec(memory_space=pltpu.SMEM)] + [vmem] * 4,
        out_specs=vmem,
        scratch_shapes=[
            pltpu.VMEM((CHUNKS, NY, toks, width), BF16),
            pltpu.VMEM((NY, 24, toks), F32),
            pltpu.VMEM((NY + 1, PEERS * TILE, 2 * toks), BF16),
            pltpu.VMEM((NY, 2 * toks, 256), BF16),
            pltpu.VMEM((CHUNKS, PEERS, block, width), BF16),
            pltpu.VMEM((CHUNKS, PEERS, block, width), BF16),
            pltpu.VMEM((TILE, PEERS * TILE), BF16),
            pltpu.VMEM((PEERS, TILE, PEERS * TILE), BF16),
            pltpu.VMEM((8, width, 2 * hidden), BF16),
            pltpu.VMEM((8, hidden, width), BF16),
            pltpu.VMEM((8, CHUNKS, rank, width), BF16),
            pltpu.VMEM((8, rank, hidden), BF16),
            pltpu.VMEM((8 * rank, 2 * hidden), BF16),
            pltpu.VMEM((PEERS // GROUP, GROUP * block, 2 * hidden + 8 * rank), F32),
            pltpu.VMEM((PEERS // GROUP, GROUP * block, hidden), BF16),
            pltpu.VMEM((CHUNKS, PEERS, block, width), BF16),
            pltpu.VMEM((CHUNKS, 4, 2, toks, width), BF16),
            pltpu.VMEM((CHUNKS, 4, 2, toks, width), BF16),
            dma((2,)),
            dma((CHUNKS, 4)),
            dma,
            dma((4,)),
            dma,
            dma((CHUNKS,)),
            dma,
            dma,
            dma((4,)),
            dma((4, 4)),
            dma,
            dma((CHUNKS, 5)),
            dma((2,)),
            dma((CHUNKS, 4)),
        ],
        compiler_params=pltpu.CompilerParams(
            collective_id=0, has_side_effects=True, vmem_limit_bytes=60 * 1024 * 1024
        ),
        cost_estimate=pl.CostEstimate(flops=8 * 10**9, bytes_accessed=3 * 10**6, transcendentals=0),
    )(
        tokens,
        chosen_expert_index.T,
        router_weight_logits.T,
        token_tenant_index[None, :],
        adapted.T,
        gate_up_weight[0],
        down_weight[0],
        adapter_input_factors[0, 0],
        adapter_output_factors[0, 0],
    )


def solution(mesh):
    placed = (
        P(("expert", "store"), None),
        P(("expert", "store"), None),
        P(("expert", "store"), None),
        P(("expert", "store")),
        P(None, "expert"),
        P("expert", "store", None),
        P("expert", None, "store"),
        P("store", "expert", None, None),
        P("store", "expert", None, None),
    )
    return jax.shard_map(
        shards, mesh=mesh, in_specs=placed, out_specs=P(("expert", "store"), None), check_vma=False
    )
```

```python
import jax
import jax.numpy as jnp
from jax import lax
from jax.experimental import pallas as pl
from jax.experimental.pallas import tpu as pltpu
from jax.sharding import PartitionSpec as P

MESH = pl.DeviceIdType.MESH
FIN, FUP, WIN, WOUT = range(4)
NX, NY, NC = 4, 8, 2
PEERS = NX * NC
SLOTS = 18
TILE = 16
CHUNKS = 8
GROUP = 4
LAG = 2
HOP = 2
STAGGER = 1
LAST_A = CHUNKS + 4 * HOP
LAST_B = CHUNKS - 1 + LAG + 4 * HOP
OWN_BACK = CHUNKS + 3 * STAGGER
PLAN_A = (
    (7, ((WIN, 1), (FIN, 1), (FUP, 1)), ((WIN, 2), (FIN, 2), (FUP, 2))),
    (10, ((WIN, 2),), ((WIN, 3),)),
    (11, ((FIN, 2), (FUP, 2)), ((FIN, 3), (FUP, 3))),
    (12, ((WIN, 3),), ((WIN, 4),)),
    (13, ((FIN, 3), (FUP, 3)), ((FIN, 4), (FUP, 4), (WOUT, 1))),
    (14, ((FIN, 4), (FUP, 4)), ()),
)
F32, BF16 = jnp.float32, jnp.bfloat16


def dot(a, b, dims=((1,), (0,))):
    return lax.dot_general(a, b, (dims, ((), ())), preferred_element_type=F32)


def chunk_column(step, z):
    far = (step + 1) // 2
    return jnp.where(step % 2 == 1, z - far + 8, z + far) % 8


def layer_kernel(
    tok_ref, idx_ref, logit_ref, ten_ref, adp_ref, win_ref, wout_ref, fin_ref, fup_ref, out_ref,
    tokbuf, meta, sel, mix, xsend, xrecv, code_s, code_r, winb, woutb, finb, fupb, wide, pre, act,
    xret, rs_s, rs_r,
    y_ss, y_rs, m_ss, m_rs, x_ss, x_rs, c_ss, c_rs, w_ss, w_rs, b_ss, b_rs, r_ss, r_rs,
):
    toks = tok_ref.shape[0]
    topk = idx_ref.shape[0]
    width = tok_ref.shape[1] // CHUNKS
    hidden = wout_ref.shape[0]
    rank = fin_ref.shape[0]
    block = NY * SLOTS
    half = toks // 2
    e = lax.axis_index("expert")
    z = lax.axis_index("store")
    x, y, c = e // (NY * NC), (e // NC) % NY, e % NC

    def at(dx, dy, dc):
        return (((x + dx) % NX * NY + (y + dy) % NY) * NC + (c + dc) % NC, z)

    def away(p):
        return at(p // NC, 0, p % NC)

    def back(p):
        return at(NX - p // NC, 0, p % NC)

    ring = (at(0, 1, 0), at(0, NY - 1, 0))
    zring = ((e, (z + 1) % 8), (e, (z + 7) % 8))

    def remote(src, dst, ss, rs, dev):
        return pltpu.make_async_remote_copy(
            src_ref=src, dst_ref=dst, send_sem=ss, recv_sem=rs, device_id=dev, device_id_type=MESH
        )

    def await_bytes(ref, sem):
        pltpu.make_async_copy(ref, ref, sem).wait()

    barrier = pltpu.get_barrier_semaphore()
    partners = [*ring, *zring] + [away(p) for p in range(1, PEERS)]
    for dev in partners:
        pl.semaphore_signal(barrier, inc=1, device_id=dev, device_id_type=MESH)

    winb[z] = win_ref[...]
    woutb[z] = wout_ref[...]
    fupb[z] = fup_ref[...]
    for k in range(CHUNKS):
        finb[z, k] = fin_ref[:, k * width : (k + 1) * width]

    def take(k, _):
        col = pl.multiple_of(chunk_column(k, z) * width, width)
        tokbuf[k, 0] = tok_ref[:, pl.ds(col, width)]
        return 0

    lax.fori_loop(0, CHUNKS, take, 0)

    ids = idx_ref[...]
    experts = NX * NY * NC
    named = lax.broadcasted_iota(jnp.int32, (experts, toks), 0)
    chosen = jnp.zeros((experts, toks), F32)
    for k in range(topk):
        chosen = chosen + jnp.where(ids[k : k + 1, :] == named, 1.0, 0.0)
    before = jnp.where(
        lax.broadcasted_iota(jnp.int32, (toks, toks), 0)
        < lax.broadcasted_iota(jnp.int32, (toks, toks), 1),
        1.0,
        0.0,
    ).astype(BF16)
    rank_of = dot(chosen.astype(BF16), before)
    peer = (((ids // (NY * NC)) - x + NX) % NX) * NC + (ids % NC + c) % NC
    place = ((ids // NC) % NY * 256 + peer * 32).astype(F32)
    for k in range(topk):
        slot = jnp.sum(jnp.where(ids[k : k + 1, :] == named, rank_of, 0.0), axis=0, keepdims=True)
        meta[0, k : k + 1, :] = place[k : k + 1, :] + slot
    logits = logit_ref[...]
    meta[0, topk : 2 * topk, :] = logits / jnp.sum(logits, axis=0, keepdims=True)
    meta[0, 2 * topk : 3 * topk, :] = jnp.broadcast_to(ten_ref[...], (topk, toks)).astype(F32)

    pl.semaphore_wait(barrier, len(partners))

    kinds = (finb, fupb, winb, woutb)

    def zsend(kind, h):
        for d in range(2):
            ref = kinds[kind].at[(z - (h - 1) + 8) % 8 if d == 0 else (z + (h - 1)) % 8]
            if h == 4:
                n = ref.shape[0] // 2
                ref = ref.at[pl.ds(d * n, n)]
            remote(ref, ref, w_ss.at[kind], w_rs.at[kind, h - 1], zring[d]).start()

    def zarrive(kind, h):
        await_bytes(kinds[kind].at[pl.ds(0, 1 if h == 4 else 2)], w_rs.at[kind, h - 1])

    def place_of(h, d):
        return 0 if h == 0 else (7 if h == 4 else 2 * h - 1 + d)

    def ysend(k, h):
        for d in range(2):
            src, dst = tokbuf.at[k, place_of(h - 1, d)], tokbuf.at[k, place_of(h, d)]
            if h == 4:
                src, dst = src.at[pl.ds(d * half, half)], dst.at[pl.ds(d * half, half)]
            remote(src, dst, y_ss.at[h // 4], y_rs.at[k, h - 1], ring[d]).start()

    def yarrive(k, h):
        await_bytes(tokbuf.at[k, pl.ds(0, 1 if h == 4 else 2)], y_rs.at[k, h - 1])

    def msend(h):
        for d in range(1 if h == 4 else 2):
            remote(meta.at[place_of(h - 1, d)], meta.at[place_of(h, d)], m_ss, m_rs.at[h - 1], ring[d]).start()

    def marrive(h):
        await_bytes(meta.at[pl.ds(0, 1 if h == 4 else 2)], m_rs.at[h - 1])

    row_no = lax.broadcasted_iota(jnp.int32, (256, toks), 0)

    def build(q):
        want = (row_no + (y * 256 - 2 * q)).astype(F32)
        hot = jnp.zeros((256, toks), F32)
        share = jnp.zeros((256, toks), F32)
        for k in range(topk):
            same = meta[q, k : k + 1, :] == want
            hot = jnp.where(same, 1.0, hot)
            share = jnp.where(same, meta[q, topk + k : topk + k + 1, :], share)
        hot = hot.astype(BF16).reshape(PEERS, 2, TILE, toks)
        sel[q, :, toks : 2 * toks] = hot[:, 0].reshape(PEERS * TILE, toks)
        sel[q + 1, :, 0:toks] = hot[:, 1].reshape(PEERS * TILE, toks)
        share = share.T
        high = share.astype(BF16)
        mix[q, 0:toks] = high
        mix[q, toks : 2 * toks] = (share - high.astype(F32)).astype(BF16)

    def tenants():
        lane_of = lax.broadcasted_iota(jnp.int32, (TILE, toks), 0)
        codes = jnp.zeros((TILE, PEERS * TILE), F32)
        for i in range(NY + 1):
            mine = lane_of == i
            if i > 0:
                v = jnp.where(mine, meta[i - 1, 2 * topk : 2 * topk + 1, :], 0.0).astype(BF16)
                codes = codes + dot(v, sel[i, :, 0:toks], ((1,), (1,)))
            if i < NY:
                v = jnp.where(mine, meta[i, 2 * topk : 2 * topk + 1, :], 0.0).astype(BF16)
                codes = codes + dot(v, sel[i, :, toks : 2 * toks], ((1,), (1,)))
        code_s[...] = codes.astype(BF16)
        code_r[0] = codes.astype(BF16)

    order = [4, 5, 2, 3, 6, 7, 1]
    tiles = {h: (max(0, 2 * h - 1), 2 * h + 1) for h in range(0, 5)}

    def rows_of(h):
        return pl.ds(tiles[h][0] * TILE, (tiles[h][1] - tiles[h][0]) * TILE)

    def select(k, h):
        for i in range(*tiles[h]):
            if i == 0:
                rows = dot(sel[0, :, toks : 2 * toks], tokbuf[k, 0])
            elif i == NY:
                rows = dot(sel[NY, :, 0:toks], tokbuf[k, NY - 1])
            else:
                rows = dot(sel[i], tokbuf[k, i - 1 : i + 1].reshape(2 * toks, width))
            rows = rows.astype(BF16).reshape(PEERS, TILE, width)
            xrecv[k, 0, i * TILE : (i + 1) * TILE] = rows[0]
            xsend[k, 1:, i * TILE : (i + 1) * TILE] = rows[1:]
        for p in order:
            remote(
                xsend.at[k, p, rows_of(h)], xrecv.at[k, p, rows_of(h)], x_ss, x_rs.at[k], away(p)
            ).start()

    def xarrive(k):
        await_bytes(xrecv.at[k, pl.ds(1, PEERS - 1)], x_rs.at[k])

    def block_rows(k, g):
        return xrecv[k, pl.ds(g * GROUP, GROUP)].reshape(GROUP * block, width)

    def accumulate(k, g):
        pre[g, :, 0 : 2 * hidden] += dot(block_rows(k, g), winb[chunk_column(k, z)])

    def lower(k, g):
        factor = finb[:, chunk_column(k, z)].reshape(8 * rank, width)
        pre[g, :, 2 * hidden :] += dot(block_rows(k, g), factor, ((1,), (1,)))

    def lower_of(first, last):
        def step(i, _):
            lower(i // 2, i % 2)
            return 0

        lax.fori_loop(2 * first, 2 * last, step, 0)

    for kind in (WIN, FIN, FUP):
        zsend(kind, 1)
    pre[...] = jnp.zeros_like(pre)

    def slot_a(t, _):
        for h in range(4, 0, -1):
            k = t - HOP * h

            @pl.when((k >= 0) & (k < CHUNKS))
            def _():
                yarrive(k, h)
                if h < 4:
                    ysend(k, h + 1)

            @pl.when(k == 0)
            def _():
                marrive(h)
                if h < 4:
                    msend(h + 1)

        @pl.when(t == 0)
        def _():
            msend(1)

        @pl.when(t < CHUNKS)
        def _():
            ysend(t, 1)

        for h in range(0, 5):

            @pl.when(t == HOP * h)
            def _():
                for q in range(max(0, 2 * h - 1), min(2 * h, 7) + 1):
                    build(q)

        for h in range(4, 0, -1):
            k = t - HOP * h

            @pl.when((k >= 0) & (k < CHUNKS))
            def _():
                select(k, h)

        @pl.when(t < CHUNKS // 2)
        def _():
            for i in range(2):
                select(2 * t + i, 0)

        @pl.when(t == 4 * HOP)
        def _():
            tenants()
            for p in order:
                remote(code_s, code_r.at[p], c_ss, c_rs, away(p)).start()

        for slot, came, goes in PLAN_A:

            @pl.when(t == slot)
            def _():
                for kind, h in came:
                    zarrive(kind, h)
                for kind, h in goes:
                    zsend(kind, h)

        @pl.when(t == LAST_A - 2)
        def _():
            lower_of(0, 4)

        @pl.when(t == LAST_A - 1)
        def _():
            lower_of(4, 6)

        done = t - 4 * HOP - 1

        @pl.when(done >= 0)
        def _():
            xarrive(done)

            def group(g, _):
                accumulate(done, g)
                return 0

            lax.fori_loop(0, PEERS // GROUP, group, 0)

        return 0

    lax.fori_loop(0, LAST_A, slot_a, 0)

    for u in range(8):
        r = u * rank
        wide[r : r + rank // 2, 0:hidden] = fupb[u, 0 : rank // 2]
        wide[r : r + rank // 2, hidden:] = jnp.zeros((rank // 2, hidden), BF16)
        wide[r + rank // 2 : r + rank, 0:hidden] = jnp.zeros((rank // 2, hidden), BF16)
        wide[r + rank // 2 : r + rank, hidden:] = fupb[u, rank // 2 :]
    zarrive(WIN, 4)
    lower_of(6, 7)
    zarrive(WOUT, 1)
    zsend(WOUT, 2)
    await_bytes(code_r.at[pl.ds(1, PEERS - 1)], c_rs)
    lane_rank = lax.broadcasted_iota(jnp.int32, (1, 8 * rank), 1) // rank
    adapted = jnp.zeros((1, 8 * rank), F32)
    for u in range(8):
        adapted = jnp.where(lane_rank == u, adp_ref[0, u].astype(F32), adapted)

    def activate(p):
        g, b = p // GROUP, (p % GROUP) * block
        rows = pl.ds(pl.multiple_of(b, block), block)
        codes = code_r[p].astype(F32)
        lane = lax.broadcasted_iota(jnp.int32, (TILE, PEERS * TILE), 1)
        mine = lane == p * TILE + lax.broadcasted_iota(jnp.int32, (TILE, PEERS * TILE), 0)
        column = jnp.concatenate(
            [
                jnp.sum(jnp.where(mine, codes[i : i + 1, :], 0.0), axis=1, keepdims=True)
                for i in range(NY + 1)
            ],
            axis=0,
        )
        of_lane = (lax.broadcasted_iota(jnp.int32, (block, 8 * rank), 1) // rank).astype(F32)
        keep = jnp.where(column == of_lane, adapted, 0.0)
        low = (pre[g, rows, 2 * hidden :] * keep).astype(BF16)
        total = pre[g, rows, 0 : 2 * hidden] + dot(low, wide[...])
        gate, up = total[:, :hidden], total[:, hidden:]
        act[g, rows] = (gate / (1.0 + jnp.exp(-gate)) * up).astype(BF16)

    await_bytes(xsend.at[:, pl.ds(1, PEERS - 1)], x_ss)

    def send_back(k, h, p):
        remote(
            xsend.at[k, p, rows_of(h)], xret.at[k, p, rows_of(h)], b_ss, b_rs.at[k, h], back(p)
        ).start()

    def returned(k, h):
        await_bytes(xret.at[k, pl.ds(1, PEERS - 1), rows_of(h)], b_rs.at[k, h])

    def rsend(k, h, d):
        src, dst = rs_s.at[k, h - 1, d], rs_r.at[k, h - 1, d]
        if h == 4:
            src, dst = src.at[pl.ds(d * half, half)], dst.at[pl.ds(d * half, half)]
        remote(src, dst, r_ss.at[h // 4], r_rs.at[k, h - 1], ring[1 - d]).start()

    def rarrive(k, h):
        await_bytes(rs_r.at[k, h - 1, pl.ds(0, 1 if h == 4 else 2)], r_rs.at[k, h - 1])

    def down(k, g):
        rows = dot(act[g], woutb[chunk_column(k, z)]).astype(BF16).reshape(GROUP, block, width)
        xsend[k, pl.ds(g * GROUP, GROUP)] = rows

        @pl.when(g == 0)
        def _():
            xret[k, 0] = rows[0]

    xarrive(CHUNKS - 1)

    def turn(i, _):
        g = 1 - i
        accumulate(CHUNKS - 1, g)
        lower(CHUNKS - 1, g)

        def one(p, _):
            activate(g * GROUP + p)
            return 0

        lax.fori_loop(0, GROUP, one, 0)
        down(0, g)
        for here in range(2):

            @pl.when(g == here)
            def _():
                for p in order:
                    if p // GROUP == here:
                        send_back(0, 4, p)

        return 0

    lax.fori_loop(0, 2, turn, 0)

    def mixed(k, q):
        rows = xret[k, :, q * TILE : (q + 2) * TILE].reshape(256, width)
        both = dot(mix[q], rows)
        return both[:toks] + both[toks:]

    def combine(k, h):
        returned(k, h)
        if h == 4:
            total = mixed(k, 7)
            for d in range(2):
                span = slice(d * half, (d + 1) * half)
                rs_s[k, 3, d, span] = total[span].astype(BF16)
                rsend(k, 4, d)
            return
        rarrive(k, h + 1)
        for d in range(2):
            total = mixed(k, place_of(h, d))
            if h == 3:
                span, rest = slice(d * half, (d + 1) * half), slice((1 - d) * half, (2 - d) * half)
                rs_s[k, 2, d, rest] = total[rest].astype(BF16)
                rs_s[k, 2, d, span] = (total[span] + rs_r[k, 3, d, span].astype(F32)).astype(BF16)
            else:
                rs_s[k, h - 1, d] = (total + rs_r[k, h, d].astype(F32)).astype(BF16)
            rsend(k, h, d)

    def finish(k):
        rarrive(k, 1)
        returned(k, 0)
        total = mixed(k, 0) + rs_r[k, 0, 0].astype(F32) + rs_r[k, 0, 1].astype(F32)
        col = pl.multiple_of(chunk_column(k, z) * width, width)
        out_ref[:, pl.ds(col, width)] = total.astype(BF16)

    def slot_b(t, _):
        for h in range(2, 5):

            @pl.when(t == 2 * h - 2)
            def _():
                zarrive(WOUT, h)
                if h < 4:
                    zsend(WOUT, h + 1)

        @pl.when((t >= 1) & (t < CHUNKS))
        def _():
            def group(g, _):
                down(t, g)
                return 0

            lax.fori_loop(0, PEERS // GROUP, group, 0)
            for p in order:
                send_back(t, 4, p)

        for h in range(3, 0, -1):
            k = t - STAGGER * (4 - h)

            @pl.when((k >= 0) & (k < CHUNKS))
            def _():
                for p in order:
                    send_back(k, h, p)

        early = t - OWN_BACK

        @pl.when((early >= 0) & (early < CHUNKS // 2))
        def _():
            for i in range(2):
                for p in order:
                    send_back(2 * early + i, 0, p)

        for h in range(1, 5):
            k = t - LAG - HOP * (4 - h)

            @pl.when((k >= 0) & (k < CHUNKS))
            def _():
                combine(k, h)

        done = t - (LAST_B - CHUNKS // 2)

        @pl.when(done >= 0)
        def _():
            finish(2 * done)
            finish(2 * done + 1)

        return 0

    lax.fori_loop(0, LAST_B, slot_b, 0)

    await_bytes(xsend.at[:, pl.ds(1, PEERS - 1)], b_ss)
    await_bytes(tokbuf.at[:, pl.ds(0, 6)], y_ss.at[0])
    await_bytes(tokbuf.at[:, 7], y_ss.at[1])
    await_bytes(rs_s.at[:, pl.ds(0, 3)], r_ss.at[0])
    await_bytes(rs_s.at[:, 3, 0], r_ss.at[1])
    await_bytes(meta.at[pl.ds(0, 7)], m_ss)
    await_bytes(code_r.at[pl.ds(1, PEERS - 1)], c_ss)
    for kind in range(4):
        await_bytes(kinds[kind].at[pl.ds(0, 7)], w_ss.at[kind])


def shards(
    tokens,
    chosen_expert_index,
    router_weight_logits,
    token_tenant_index,
    adapted,
    gate_up_weight,
    down_weight,
    adapter_input_factors,
    adapter_output_factors,
):
    toks, model = tokens.shape
    width = model // CHUNKS
    hidden = down_weight.shape[1]
    rank = adapter_input_factors.shape[2]
    block = NY * SLOTS
    vmem = pl.BlockSpec(memory_space=pltpu.VMEM)
    dma = pltpu.SemaphoreType.DMA
    return pl.pallas_call(
        layer_kernel,
        out_shape=jax.ShapeDtypeStruct((toks, model), BF16),
        in_specs=[vmem] * 4 + [pl.BlockSpec(memory_space=pltpu.SMEM)] + [vmem] * 4,
        out_specs=vmem,
        scratch_shapes=[
            pltpu.VMEM((CHUNKS, NY, toks, width), BF16),
            pltpu.VMEM((NY, 24, toks), F32),
            pltpu.VMEM((NY + 1, PEERS * TILE, 2 * toks), BF16),
            pltpu.VMEM((NY, 2 * toks, 256), BF16),
            pltpu.VMEM((CHUNKS, PEERS, block, width), BF16),
            pltpu.VMEM((CHUNKS, PEERS, block, width), BF16),
            pltpu.VMEM((TILE, PEERS * TILE), BF16),
            pltpu.VMEM((PEERS, TILE, PEERS * TILE), BF16),
            pltpu.VMEM((8, width, 2 * hidden), BF16),
            pltpu.VMEM((8, hidden, width), BF16),
            pltpu.VMEM((8, CHUNKS, rank, width), BF16),
            pltpu.VMEM((8, rank, hidden), BF16),
            pltpu.VMEM((8 * rank, 2 * hidden), BF16),
            pltpu.VMEM((PEERS // GROUP, GROUP * block, 2 * hidden + 8 * rank), F32),
            pltpu.VMEM((PEERS // GROUP, GROUP * block, hidden), BF16),
            pltpu.VMEM((CHUNKS, PEERS, block, width), BF16),
            pltpu.VMEM((CHUNKS, 4, 2, toks, width), BF16),
            pltpu.VMEM((CHUNKS, 4, 2, toks, width), BF16),
            dma((2,)),
            dma((CHUNKS, 4)),
            dma,
            dma((4,)),
            dma,
            dma((CHUNKS,)),
            dma,
            dma,
            dma((4,)),
            dma((4, 4)),
            dma,
            dma((CHUNKS, 5)),
            dma((2,)),
            dma((CHUNKS, 4)),
        ],
        compiler_params=pltpu.CompilerParams(
            collective_id=0, has_side_effects=True, vmem_limit_bytes=60 * 1024 * 1024
        ),
        cost_estimate=pl.CostEstimate(flops=8 * 10**9, bytes_accessed=3 * 10**6, transcendentals=0),
    )(
        tokens,
        chosen_expert_index.T,
        router_weight_logits.T,
        token_tenant_index[None, :],
        adapted.T,
        gate_up_weight[0],
        down_weight[0],
        adapter_input_factors[0, 0],
        adapter_output_factors[0, 0],
    )


def solution(mesh):
    placed = (
        P(("expert", "store"), None),
        P(("expert", "store"), None),
        P(("expert", "store"), None),
        P(("expert", "store")),
        P(None, "expert"),
        P("expert", "store", None),
        P("expert", None, "store"),
        P("store", "expert", None, None),
        P("store", "expert", None, None),
    )
    return jax.shard_map(
        shards, mesh=mesh, in_specs=placed, out_specs=P(("expert", "store"), None), check_vma=False
    )
```
